512 devices in a mesh: sector: 32 (over z, core), slab: 16 (over x, y).
Axes of the slice: x: 4, y: 4, z: 16, core: 2. Of those that a mesh axis runs over, the one named last changes fastest.
Arguments:
- image: float32 [48, 64, 128], P('slab', 'sector'), may hold values from 0.2 to 2
- sensitivity: float32 [48, 64, 128], P('slab', 'sector'), may hold values from 0.01 to 0.1
- tile_values: bfloat16 [32, 192, 104, 256], P('sector', 'slab'), may hold values from 0.049804688 to 1
- tile_rows: int32 [32, 192], P('sector', 'slab'), may hold values from 0 to 31
- tile_cols: int32 [32, 192], P('sector', 'slab'), may hold values from 0 to 95
- tile_count: int32 [32, 16], P('sector', 'slab'), may hold values from 2 to 12, as said below
- measured: float32 [32, 32, 104], P('sector'), may hold values from 0 to 3
- background: float32 [32, 32, 104], P('sector'), may hold values from 0.2 to 1
- w_in: bfloat16 [32, 1, 3, 3, 3], replicated, may hold values from -1.25 to 1.25
- w_mid: bfloat16 [3, 32, 32, 3, 3, 3], replicated, may hold values from -0.21875 to 0.21875
- w_out: bfloat16 [1, 32, 3, 3, 3], replicated, may hold values from -0.21875 to 0.21875
- cotangent: float32 [48, 64, 128], P('slab', 'sector'), may hold values from -36 to 36
Outputs:
- new_image: float32 [48, 64, 128], P('slab', 'sector')
- em_grad: float32 [48, 64, 128], P('slab', 'sector')
- grad_in: float32 [32, 1, 3, 3, 3], replicated
- grad_mid: float32 [3, 32, 32, 3, 3, 3], replicated
- grad_out: float32 [1, 32, 3, 3, 3], replicated
The draws below stay inside these ranges and needn't reach their ends.
Inputs may be any that keep to these rules, and one draw needn't show every extreme that they name: `tile_rows`: row block of a sector, of 32. `tile_cols`: voxel block of a slab, of 96. The first tile_count slots of a device are used; some device uses all 12 in every draw.
All inputs are finite; a program needn't handle non-finite values.
Results may differ from the reference program's by a relative error of at most 0.0085.
The reference program's roundings to bfloat16 on the way count: a program that leaves them out, or rounds other values in their place, can miss the bound.
Values may be sent and summed in bfloat16 or wider, within the bound.
No kernel may reach another device: no remote copies, remote signals or barrier semaphores. Data moves between devices by JAX's collectives and lax.ppermute only.
A program may use at most 64 MiB of HBM per device.

```python
import math
import jax
import jax.numpy as jnp
from jax import lax

C = 32
MID = 3
KMAX = 12
XS = 2
Y = 128
ZS = 3
RB = 104
VB = 256
SECTORS = 32
SLABS = 16
NLB = 32
NVB = 96
X = 64
Z = 48


def draw_tile_count(key, part):
    key = jax.random.fold_in(key, 11)
    key_base, key_busy, key_pick = jax.random.split(key, 3)
    baseline = jax.random.randint(key_base, (SECTORS, SLABS), 2, KMAX // 2 + 1)
    crowded = jax.random.randint(key_busy, (SECTORS, SLABS), 0, 8) == 0
    counts = jnp.where(crowded, KMAX, baseline).reshape(-1)
    chosen = jax.random.randint(key_pick, (), 0, SECTORS * SLABS)
    return counts.at[chosen].set(KMAX).reshape(SECTORS, SLABS).astype(jnp.int32)


def draw_cotangent(key, part):
    key = jax.random.fold_in(key, 5)
    depth_ramp = 1.0 + 2.0 * jnp.arange(Z, dtype=jnp.float32)[:, None, None] / (Z - 1)
    row_ramp = 1.0 + 2.0 * jnp.arange(X, dtype=jnp.float32)[None, :, None] / (X - 1)
    noise = jnp.clip(jax.random.normal(key, (Z, X, Y), jnp.float32), -4.0, 4.0)
    return (noise * depth_ramp * row_ramp).astype(jnp.float32)


def with_ends(drawn, own_key, smallest, largest):
    spot = [jax.random.randint(jax.random.fold_in(own_key, axis), (), 0, length) for axis, length in enumerate(drawn.shape)]
    widest = drawn.shape.index(max(drawn.shape))
    next_to = spot[:widest] + [(spot[widest] + 1) % drawn.shape[widest]] + spot[widest + 1:]
    return drawn.at[tuple(spot)].set(smallest).at[tuple(next_to)].set(largest)


def level_of(stream_key, extent, shards, smallest, high):
    factor_of = 1.0
    for position, shards_of in shards:
        draws = jax.random.uniform(jax.random.fold_in(jax.random.fold_in(stream_key, 6), position), (shards_of,), jnp.float32, smallest / len(shards), high / len(shards))
        factor_of = factor_of * jnp.repeat(jnp.exp(draws), extent[position] // shards_of).reshape((-1,) + (1,) * (len(extent) - 1 - position))
    return factor_of


def gaussian(stream_key, shape, scale, bound, kind=jnp.bfloat16):
    entries = jax.random.normal(stream_key, shape, jnp.float32) * scale
    return jnp.minimum(jnp.maximum(entries, -bound), bound).astype(kind)


def setup_inputs(seed: int = 0) -> dict:
    keys = jax.random.split(jax.random.key(seed), 13)
    image = jnp.clip(jnp.exp(math.log(2.0) - 2.3025851 * jax.random.uniform(keys[0], (Z, X, Y), jnp.float32) ** level_of(keys[0], (Z, X, Y), ((0, 16), (1, 32)), -0.2, 0.2)), 0.2, 2.0)
    sensitivity = jnp.clip(jnp.exp(math.log(0.1) - 2.3025851 * jax.random.uniform(keys[1], (Z, X, Y), jnp.float32) ** level_of(keys[1], (Z, X, Y), ((0, 16), (1, 32)), -0.2, 0.2)), 0.01, 0.1)
    tile_values = jnp.clip(jnp.exp(math.log(1.0) - 2.9996462 * jax.random.uniform(keys[2], (SECTORS, SLABS * KMAX, RB, VB), jnp.float32) ** level_of(keys[2], (SECTORS, SLABS * KMAX, RB, VB), ((0, 32), (1, 16)), -0.2, 0.2)), 0.049804688, 1.0).astype(jnp.bfloat16)
    tile_rows = with_ends(jax.random.randint(keys[3], (SECTORS, SLABS * KMAX), 0, NLB), jax.random.fold_in(keys[3], 1), 0, NLB - 1).astype(jnp.int32)
    tile_cols = with_ends(jax.random.randint(keys[4], (SECTORS, SLABS * KMAX), 0, NVB), jax.random.fold_in(keys[4], 1), 0, NVB - 1).astype(jnp.int32)
    tile_count = draw_tile_count(jax.random.fold_in(keys[12], 71), 0)
    measured = jnp.clip(3.0 * jax.random.uniform(keys[6], (SECTORS, NLB, RB), jnp.float32) ** level_of(keys[6], (SECTORS, NLB, RB), ((0, 32),), -0.2, 0.2), 0.0, 3.0)
    background = jnp.clip(0.2 + 0.8 * jax.random.uniform(keys[7], (SECTORS, NLB, RB), jnp.float32) ** level_of(keys[7], (SECTORS, NLB, RB), ((0, 32),), -0.2, 0.2), 0.2, 1.0)
    w_in = gaussian(keys[8], (C, 1, 3, 3, 3), 27 ** -0.5, 1.25)
    w_mid = gaussian(keys[9], (MID, C, C, 3, 3, 3), (27 * C) ** -0.5, 0.21875)
    w_out = gaussian(keys[10], (1, C, 3, 3, 3), (27 * C) ** -0.5, 0.21875)
    cotangent = draw_cotangent(jax.random.fold_in(keys[12], 71), 0)
    return dict(image=image, sensitivity=sensitivity, tile_values=tile_values, tile_rows=tile_rows, tile_cols=tile_cols, tile_count=tile_count, measured=measured, background=background, w_in=w_in, w_mid=w_mid, w_out=w_out, cotangent=cotangent)


def conv_valid(padded, kernel):
    result = lax.conv_general_dilated(padded[None], kernel, (1, 1, 1), 'VALID', dimension_numbers=('NCDHW', 'OIDHW', 'NCDHW'), preferred_element_type=jnp.float32)
    return result[0]

def flipped(kernel):
    return jnp.transpose(jnp.flip(kernel, (2, 3, 4)), (1, 0, 2, 3, 4))

def weight_grad(padded, cotan):
    result = lax.conv_general_dilated(padded[:, None], cotan[:, None], (1, 1, 1), 'VALID', dimension_numbers=('NCDHW', 'OIDHW', 'NCDHW'), preferred_element_type=jnp.float32)
    return jnp.transpose(result, (1, 0, 2, 3, 4))

def silu_slope(preact):
    sigma = jax.nn.sigmoid(preact)
    return sigma * (1.0 + preact * (1.0 - sigma))

def pad_whole(field):
    return jnp.pad(field, ((0, 0), (1, 1), (1, 1), (1, 1)))

def network(em_image, w_in, w_mid, w_out, cotangent, extend):
    padded = [extend(em_image.astype(jnp.bfloat16)[None])]
    preacts = []
    kernels = [w_in] + [w_mid[layer] for layer in range(w_mid.shape[0])]
    for kernel in kernels:
        preact = conv_valid(padded[-1], kernel)
        preacts.append(preact)
        padded.append(extend(jax.nn.silu(preact).astype(jnp.bfloat16)))
    new_image = em_image + conv_valid(padded[-1], w_out)[0]
    cotan = cotangent.astype(jnp.bfloat16)[None]
    grad_out = weight_grad(padded[-1], cotan)
    back_kernel = w_out
    grads = []
    for layer in range(len(kernels) - 1, -1, -1):
        inward = conv_valid(extend(cotan), flipped(back_kernel))
        cotan = (silu_slope(preacts[layer]) * inward).astype(jnp.bfloat16)
        grads.append(weight_grad(padded[layer], cotan))
        back_kernel = kernels[layer]
    em_grad = cotangent + conv_valid(extend(cotan), flipped(w_in))[0]
    grads = grads[::-1]
    return (new_image, em_grad, grads[0], jnp.stack(grads[1:]), grad_out)

def reference(image, sensitivity, tile_values, tile_rows, tile_cols, tile_count, measured, background, w_in, w_mid, w_out, cotangent):
    block_len = XS * Y
    slab_blocks = image.astype(jnp.bfloat16).reshape(SLABS, ZS * SECTORS, block_len)
    slab_index = jnp.arange(SLABS)[:, None]
    slot_index = jnp.arange(KMAX)[None, :]
    highest = lax.Precision.HIGHEST

    def sector_step(carry_total, pieces):
        values_here, rows_here, cols_here, count_here, measured_here, background_here = pieces
        values_here = values_here.reshape(SLABS, KMAX, RB, block_len).astype(jnp.float32)
        rows_here = rows_here.reshape(SLABS, KMAX)
        cols_here = cols_here.reshape(SLABS, KMAX)
        weights_here = (slot_index < count_here[:, None]).astype(jnp.float32) / block_len
        picked = slab_blocks[slab_index, cols_here].astype(jnp.float32)
        forward = jnp.einsum('pkrv,pkv->pkr', values_here, picked, precision=highest) * weights_here[:, :, None]
        projection = jnp.zeros((NLB, RB), jnp.float32).at[rows_here.reshape(-1)].add(forward.reshape(-1, RB))
        ratio = (measured_here / (projection + background_here)).astype(jnp.bfloat16)
        ratio_rows = ratio[rows_here].astype(jnp.float32)
        backward = jnp.einsum('pkrv,pkr->pkv', values_here, ratio_rows, precision=highest) * weights_here[:, :, None]
        return (carry_total.at[slab_index, cols_here].add(backward), None)
    start_total = jnp.zeros((SLABS, ZS * SECTORS, block_len), jnp.float32)
    total, _ = lax.scan(sector_step, start_total, (tile_values, tile_rows, tile_cols, tile_count, measured, background))
    back_image = total.reshape(Z, X, Y)
    em_image = image * back_image / sensitivity
    new_image, em_grad, grad_in, grad_mid, grad_out = network(em_image, w_in, w_mid, w_out, cotangent, pad_whole)
    factor = 1.0 / math.sqrt(Z * X * Y)
    return (new_image, em_grad, grad_in * factor, grad_mid * factor, grad_out * factor)
```

```python
import math

import jax
import jax.numpy as jnp
from jax import lax
from jax.experimental import pallas as pl
from jax.experimental.pallas import tpu as pltpu
from jax.sharding import PartitionSpec as P

LANES = 128
VMEM_BYTES = 56 * 1024 * 1024


class Plan:
    def __init__(self, zs, xs, channels, layers):
        self.zs, self.xs, self.c, self.layers = zs, xs, channels, layers
        self.halo_u = [2 * layers - l + 1 for l in range(1, layers + 2)]
        self.halo_c = [l for l in range(1, layers + 1)]
        self.halo_in = 2 * layers
        self.halo_last = layers + 1
        self.lead_in = -(self.halo_in - 1) % 8
        self.lead_last = -(self.halo_last - 1) % 8
        self.rows_in = -(-(zs + 2 * self.halo_in + self.lead_in) // 8) * 8
        self.rows_last = -(-(zs + 2 * self.halo_last + self.lead_last) // 8) * 8

    def z(self, halo):
        return self.zs + 2 * halo

    def x(self, halo):
        return self.xs + 2 * halo

    def starts(self, planes):
        count = -(-planes // 6)
        size = -(-planes // count)
        return size, [min(k * size, planes - size) for k in range(count)]


def round_up(value, step):
    return -(-value // step) * step


def shifts(rows):
    lane = lax.broadcasted_iota(jnp.int32, rows.shape, 1)
    low = jnp.where(lane == 0, 0.0, pltpu.roll(rows, 1, 1))
    high = jnp.where(lane == LANES - 1, 0.0, pltpu.roll(rows, LANES - 1, 1))
    return low, rows, high


def prepare_kernel(plan, base_in, base_last, base_out, base_back, *refs):
    mids = 2 * (plan.layers - 1)
    bases, outs = refs[:mids], refs[mids:]
    w_first, w_top, w_out, w_back = outs[:4]
    toeplitz = outs[4:]
    c = plan.c
    for base, out, step, planes in (
        (base_in, w_first, 1, plan.z(plan.halo_u[1])),
        (base_last, w_top, 1, plan.z(plan.halo_c[-1])),
    ):
        rows = base[...].astype(jnp.float32)
        for k in range(planes):
            moved = rows if k == 0 else pltpu.roll(rows, k * step, 1)
            out[k * c : (k + 1) * c, :] = moved.astype(jnp.bfloat16)
    for base, out in ((base_out, w_out), (base_back, w_back)):
        rows = base[...].astype(jnp.float32)
        line = lax.broadcasted_iota(jnp.int32, rows.shape, 0)
        total = jnp.where(line == 0, rows, 0.0)
        for k in range(1, plan.zs):
            total = total + jnp.where(line == k, pltpu.roll(rows, k * c, 1), 0.0)
        out[...] = total.astype(jnp.bfloat16)
    for base, out in zip(bases, toeplitz):
        rows = base[...].astype(jnp.float32)
        for k in range(out.shape[0] // c):
            moved = rows if k == 0 else pltpu.roll(rows, k * c, 1)
            out[k * c : (k + 1) * c, :] = moved.astype(jnp.bfloat16)


def inside(first, count, c, bound):
    line = lax.broadcasted_iota(jnp.int32, (count * c, 1), 0)
    plane = first + lax.shift_right_arithmetic(line, int(math.log2(c)))
    return jnp.logical_and(plane >= 0, plane < bound)


def network_kernel(plan, grid, pos, u_first, c_last, em_own, cot_own, w_first, w_top, w_out, w_back, *refs):
    layers, c, zs, xs = plan.layers, plan.c, plan.zs, plan.xs
    mids = layers - 1
    w_fwd, w_bwd = refs[:mids], refs[mids : 2 * mids]
    new_image, em_grad, grads = refs[2 * mids : 2 * mids + 3]
    scratch = refs[2 * mids + 3 :]
    first_sh, last_sh = scratch[:2]
    u_sh = scratch[2 : 2 + layers]
    pre = scratch[2 + layers : 2 + 2 * layers]
    c_sh = scratch[2 + 2 * layers : 2 + 3 * layers]
    z_first, x_first = pos[0], pos[1]
    f32, bf16 = jnp.float32, jnp.bfloat16

    for source, target, count in (
        (u_first, first_sh, plan.x(plan.halo_in)),
        (c_last, last_sh, plan.x(plan.halo_last)),
    ):
        for k in range(count):
            span = slice(k * LANES, (k + 1) * LANES)
            for dy, rows in enumerate(shifts(source[:, span].astype(f32))):
                target[dy, :, span] = rows

    def store_shifted(target, value, rows, lane, x_at, keep):
        for half in range(2):
            part = value[:, half * LANES : (half + 1) * LANES]
            good = jnp.logical_and(x_at + half >= 0, x_at + half < grid[1])
            part = jnp.where(jnp.logical_and(keep, good), part, 0.0)
            for dy, moved in enumerate(shifts(part)):
                target[dy, rows, pl.ds(lane + half * LANES, LANES)] = moved.astype(bf16)

    def one_channel(source, weight, lane):
        pieces = [
            source[dy, :, pl.ds(lane + dx * LANES, 2 * LANES)] for dx in range(3) for dy in range(3)
        ]
        stacked = jnp.concatenate(pieces, axis=0).astype(bf16)
        return jnp.dot(weight[:, : stacked.shape[0]], stacked, preferred_element_type=f32)

    def many_channels(source, weight, first_plane, planes, lane):
        rows = slice(first_plane * c, (first_plane + planes + 2) * c)
        pieces = [
            source[dy, rows, pl.ds(lane + dx * LANES, 2 * LANES)]
            for dx in range(3)
            for dy in range(3)
        ]
        stacked = jnp.concatenate(pieces, axis=0)
        return jnp.dot(weight[:, : stacked.shape[0]], stacked, preferred_element_type=f32)

    def forward_tail(value, layer, first_plane, planes, pair, lane):
        halo = plan.halo_u[layer]
        rows = slice(first_plane * c, (first_plane + planes) * c)
        pre[layer - 1][rows, pl.ds(lane, 2 * LANES)] = value
        act = value * jax.nn.sigmoid(value)
        keep = inside(z_first - halo + first_plane, planes, c, grid[0])
        store_shifted(u_sh[layer - 1], act, rows, lane, x_first - halo + 2 * pair, keep)

    def backward_tail(value, layer, first_plane, planes, pair, lane):
        halo, halo_pre = plan.halo_c[layer - 1], plan.halo_u[layer]
        rows = slice(first_plane * c, (first_plane + planes) * c)
        from_plane = first_plane + halo_pre - halo
        preact = pre[layer - 1][
            from_plane * c : (from_plane + planes) * c,
            pl.ds(lane + (halo_pre - halo) * LANES, 2 * LANES),
        ]
        sigma = jax.nn.sigmoid(preact)
        slope = sigma * (1.0 + preact * (1.0 - sigma))
        keep = inside(z_first - halo + first_plane, planes, c, grid[0])
        store_shifted(
            c_sh[layer - 1], slope * value, rows, lane, x_first - halo + 2 * pair, keep
        )

    def over_pairs(count, body):
        def step(pair, carry):
            body(pair, pl.multiple_of(pair * 2 * LANES, 2 * LANES))
            return carry

        lax.fori_loop(0, count, step, 0)

    halo = plan.halo_u[1]

    def first_layer(pair, lane):
        value = one_channel(first_sh, w_first, lane)
        forward_tail(value, 1, 0, plan.z(halo), pair, lane)

    over_pairs(plan.x(halo) // 2, first_layer)
    for layer in range(2, layers + 1):
        halo = plan.halo_u[layer]
        size, starts = plan.starts(plan.z(halo))
        for start in starts:

            def middle(pair, lane, layer=layer, size=size, start=start):
                value = many_channels(u_sh[layer - 2], w_fwd[layer - 2], start, size, lane)
                forward_tail(value, layer, start, size, pair, lane)

            over_pairs(plan.x(halo) // 2, middle)

    def own_taps(source, halo):
        rows = slice((halo - 1) * c, (halo + zs + 1) * c)
        pieces = [
            source[dy, rows, (halo - 1 + dx) * LANES : (halo - 1 + dx + xs) * LANES]
            for dx in range(3)
            for dy in range(3)
        ]
        return jnp.concatenate(pieces, axis=0)

    top = plan.halo_u[layers]
    taps = own_taps(u_sh[layers - 1], top)
    last = jnp.dot(w_out[:, : taps.shape[0]], taps, preferred_element_type=f32)
    new_image[...] = em_own[...] + last[:zs, :]

    halo = plan.halo_c[-1]

    def top_layer(pair, lane):
        value = one_channel(last_sh, w_top, lane)
        backward_tail(value, layers, 0, plan.z(halo), pair, lane)

    over_pairs(plan.x(halo) // 2, top_layer)
    for layer in range(layers - 1, 0, -1):
        halo = plan.halo_c[layer - 1]
        size, starts = plan.starts(plan.z(halo))
        for start in starts:

            def middle_back(pair, lane, layer=layer, size=size, start=start):
                value = many_channels(c_sh[layer], w_bwd[layer - 1], start, size, lane)
                backward_tail(value, layer, start, size, pair, lane)

            over_pairs(plan.x(halo) // 2, middle_back)
    taps = own_taps(c_sh[0], plan.halo_c[0])
    down = jnp.dot(w_back[:, : taps.shape[0]], taps, preferred_element_type=f32)
    em_grad[...] = cot_own[...] + down[:zs, :]

    def own_rows(source, halo, plane):
        return source[1, (halo + plane) * c : (halo + plane + 1) * c, halo * LANES : (halo + xs) * LANES]

    def against(cells, taps):
        return lax.dot_general(cells, taps, (((1,), (1,)), ((), ())), preferred_element_type=f32)

    block = round_up(27 * c, LANES)
    grads[...] = jnp.zeros(grads.shape, f32)
    for layer in range(2, layers + 1):
        source, halo = u_sh[layer - 2], plan.halo_u[layer - 1]
        total = None
        for plane in range(zs):
            rows = slice((halo - 1 + plane) * c, (halo + 2 + plane) * c)
            pieces = [
                source[dy, rows, (halo - 1 + dx) * LANES : (halo - 1 + dx + xs) * LANES]
                for dx in range(3)
                for dy in range(3)
            ]
            cells = own_rows(c_sh[layer - 1], plan.halo_c[layer - 1], plane)
            term = against(cells, jnp.concatenate(pieces, axis=0))
            total = term if total is None else total + term
        grads[:, (layer - 2) * block : (layer - 2) * block + 27 * c] = total

    def thin(source, halo, lead, cells_of, at):
        row = lead + halo - 1
        pieces = [
            source[dy, row : row + 8, (halo - 1 + dx) * LANES : (halo - 1 + dx + xs) * LANES]
            for dx in range(3)
            for dy in range(3)
        ]
        pieces.append(jnp.zeros((LANES - 72, xs * LANES), f32))
        taps = jnp.concatenate(pieces, axis=0).astype(bf16)
        total = None
        for plane in range(zs):
            term = against(cells_of(plane), taps)
            if plane:
                term = pltpu.roll(term, LANES - plane, 1)
            total = term if total is None else total + term
        grads[:, at : at + LANES] = total

    thin(
        first_sh,
        plan.halo_in,
        plan.lead_in,
        lambda plane: own_rows(c_sh[0], plan.halo_c[0], plane),
        mids * block,
    )
    thin(
        last_sh,
        plan.halo_last,
        plan.lead_last,
        lambda plane: own_rows(u_sh[layers - 1], top, plane),
        mids * block + LANES,
    )


def toeplitz_bases(plan, w_in, w_mid, w_out):
    c, layers = plan.c, plan.layers
    mids = w_mid.shape[0]

    def spread(weights, planes, lead=0):
        moved = jnp.transpose(weights, (0, 2, 3, 1, 4))
        moved = jnp.pad(moved, ((0, 0), (0, 0), (0, 0), (lead, planes - 3 - lead), (0, 0)))
        flat = moved.reshape(weights.shape[0], 9 * planes * weights.shape[4])
        return jnp.pad(flat, ((0, 0), (0, round_up(flat.shape[1], LANES) - flat.shape[1])))

    first = jnp.transpose(w_in, (0, 2, 3, 4, 1))
    base_in = spread(first, plan.rows_in, plan.lead_in)
    last_back = jnp.transpose(jnp.flip(w_out, (2, 3, 4)), (1, 2, 3, 4, 0))
    base_last = spread(last_back, plan.rows_last, plan.lead_last)
    out_fwd = jnp.transpose(w_out, (0, 2, 3, 4, 1))
    in_back = jnp.transpose(jnp.flip(w_in, (2, 3, 4)), (1, 2, 3, 4, 0))
    base_out = jnp.broadcast_to(spread(out_fwd, plan.zs + 2), (8, round_up(9 * (plan.zs + 2) * c, LANES)))
    base_back = jnp.broadcast_to(spread(in_back, plan.zs + 2), base_out.shape)
    bases, sizes = [], []
    forward = jnp.transpose(w_mid, (0, 1, 3, 4, 5, 2))
    backward = jnp.transpose(jnp.flip(w_mid, (3, 4, 5)), (0, 2, 3, 4, 5, 1))
    for k in range(mids):
        size, _ = plan.starts(plan.z(plan.halo_u[k + 2]))
        bases.append(spread(forward[k], size + 2))
        sizes.append(size)
    for k in range(mids):
        size, _ = plan.starts(plan.z(plan.halo_c[k]))
        bases.append(spread(backward[k], size + 2))
        sizes.append(size)
    return (base_in, base_last, base_out, base_back, *bases), sizes


def prepared_weights(plan, w_in, w_mid, w_out):
    bases, sizes = toeplitz_bases(plan, w_in, w_mid, w_out)
    c, bf16 = plan.c, jnp.bfloat16
    shapes = [
        (plan.z(plan.halo_u[1]) * c, bases[0].shape[1]),
        (plan.z(plan.halo_c[-1]) * c, bases[1].shape[1]),
        bases[2].shape,
        bases[3].shape,
    ]
    shapes += [(size * c, base.shape[1]) for size, base in zip(sizes, bases[4:])]
    vmem = pl.BlockSpec(memory_space=pltpu.VMEM)
    return pl.pallas_call(
        lambda *refs: prepare_kernel(plan, *refs),
        out_shape=[jax.ShapeDtypeStruct(shape, bf16) for shape in shapes],
        in_specs=[vmem] * len(bases),
        out_specs=[vmem] * len(shapes),
        compiler_params=pltpu.CompilerParams(vmem_limit_bytes=VMEM_BYTES),
        name="prepare_weights",
    )(*bases)


def network(plan, grid, z_first, x_first, u_first, c_last, em_own, cot_own, weights):
    layers, c = plan.layers, plan.c
    f32, bf16 = jnp.float32, jnp.bfloat16
    block = round_up(27 * c, LANES)
    width = (layers - 1) * block + 2 * LANES
    own = jax.ShapeDtypeStruct((plan.zs, plan.xs * LANES), f32)
    scratch = [
        pltpu.VMEM((3, plan.rows_in, plan.x(plan.halo_in) * LANES), f32),
        pltpu.VMEM((3, plan.rows_last, plan.x(plan.halo_last) * LANES), f32),
    ]

    def region(halo, lead=()):
        return (*lead, plan.z(halo) * c, plan.x(halo) * LANES)

    scratch += [pltpu.VMEM(region(plan.halo_u[l], (3,)), bf16) for l in range(1, layers + 1)]
    scratch += [pltpu.VMEM(region(plan.halo_u[l]), f32) for l in range(1, layers + 1)]
    scratch += [pltpu.VMEM(region(plan.halo_c[l - 1], (3,)), bf16) for l in range(1, layers + 1)]
    vmem = pl.BlockSpec(memory_space=pltpu.VMEM)
    position = jnp.stack([z_first, x_first]).astype(jnp.int32)
    operands = (position, u_first, c_last, em_own, cot_own, *weights)
    return pl.pallas_call(
        lambda *refs: network_kernel(plan, grid, *refs),
        out_shape=[own, own, jax.ShapeDtypeStruct((c, width), f32)],
        in_specs=[pl.BlockSpec(memory_space=pltpu.SMEM)] + [vmem] * (len(operands) - 1),
        out_specs=[vmem] * 3,
        scratch_shapes=scratch,
        compiler_params=pltpu.CompilerParams(vmem_limit_bytes=VMEM_BYTES),
        name="network",
    )(*operands)


def unpack_grads(plan, packed):
    c, mids = plan.c, plan.layers - 1
    block = round_up(27 * c, LANES)
    mid = packed[:, : mids * block].reshape(c, mids, block)[:, :, : 27 * c]
    mid = mid.reshape(c, mids, 3, 3, 3, c)
    mid = jnp.transpose(mid, (1, 0, 5, 4, 2, 3))
    thin = packed[:, mids * block :].reshape(c, 2, LANES)[:, :, :72].reshape(c, 2, 3, 3, 8)[..., :3]
    thin = jnp.transpose(thin, (1, 0, 4, 2, 3))
    grad_in = thin[0][:, None]
    grad_out = jnp.flip(thin[1], (1, 2, 3))[None]
    return grad_in, mid, grad_out


def shards(
    image,
    sensitivity,
    tile_values,
    tile_rows,
    tile_cols,
    tile_count,
    measured,
    background,
    w_in,
    w_mid,
    w_out,
    cotangent,
):
    f32, bf16 = jnp.float32, jnp.bfloat16
    highest = lax.Precision.HIGHEST
    sectors, slabs = lax.axis_size("sector"), lax.axis_size("slab")
    sector, slab = lax.axis_index("sector"), lax.axis_index("slab")
    zs, xs, ys = image.shape
    block_len = xs * ys
    line_blocks, row_len = measured.shape[1:]
    slots = tile_rows.shape[1]
    plan = Plan(zs, xs, w_in.shape[0], w_mid.shape[0] + 1)
    grid = (zs * slabs, xs * sectors)

    weights = prepared_weights(plan, w_in, w_mid, w_out)

    cols_row = jnp.pad(tile_cols.astype(f32), ((0, 0), (0, block_len - slots))).reshape(1, xs, ys)
    sent = jnp.concatenate([image, sensitivity, cotangent, cols_row], axis=0)
    got = lax.all_gather(sent, "sector", axis=1, tiled=True)
    image_slab, sens_slab, cot_slab = got[:zs], got[zs : 2 * zs], got[2 * zs : 3 * zs]
    every_cols = got[3 * zs].reshape(sectors, block_len)[:, :slots].reshape(-1)

    values = tile_values[0]
    weight = (jnp.arange(slots) < tile_count[0, 0]).astype(f32) / block_len
    blocks = image_slab.astype(bf16).reshape(zs * sectors, block_len)
    forward = jnp.einsum("krv,kv->kr", values, blocks[tile_cols[0]], preferred_element_type=f32)
    forward = forward * weight[:, None]
    lined = jnp.concatenate([forward, tile_rows[0].astype(f32)[:, None]], axis=1)
    lined = jnp.pad(lined, ((0, 0), (0, LANES - row_len - 1)))
    every = lax.all_gather(lined, "slab", axis=0, tiled=True)
    every_rows = every[:, row_len]
    placing = (every_rows[None, :] == jnp.arange(line_blocks, dtype=f32)[:, None]).astype(f32)
    projection = jnp.dot(placing, every[:, :row_len], precision=highest)
    ratio = (measured[0] / (projection + background[0])).astype(bf16)

    backward = jnp.einsum("krv,kr->kv", values, ratio[tile_rows[0]], preferred_element_type=f32)
    backward = backward * weight[:, None]
    every_back = lax.all_gather(backward, "sector", axis=0, tiled=True)
    reach = -(-plan.halo_in // xs)
    near = sector - reach + jnp.arange(2 * reach + 1)
    wanted = (jnp.arange(zs)[:, None] * sectors + near[None, :]).astype(f32)
    good = jnp.logical_and(near >= 0, near < sectors)
    wanted = jnp.where(good[None, :], wanted, -1.0).reshape(-1)
    owning = (every_cols[None, :] == wanted[:, None]).astype(f32)
    halo = plan.halo_in
    back = jnp.dot(owning, every_back, precision=highest).reshape(zs, xs * (2 * reach + 1), ys)
    back = back[:, reach * xs - halo : reach * xs + xs + halo]

    def window(field, halo, fill):
        padded = jnp.pad(field, ((0, 0), (halo, halo), (0, 0)), constant_values=fill)
        return lax.dynamic_slice_in_dim(padded, sector * xs, xs + 2 * halo, 1)

    em = window(image_slab, halo, 0.0) * back / window(sens_slab, halo, 1.0)
    em_own = em[:, halo : halo + xs]

    cot_wide = window(cot_slab, plan.halo_last, 0.0).astype(bf16)
    both = jnp.concatenate([em.astype(bf16), cot_wide], axis=1)
    every_plane = lax.all_gather(both, "slab", axis=0, tiled=True)

    def planes(lo, count, halo, lead, rows):
        field = every_plane[:, lo : lo + count]
        padded = jnp.pad(field, ((halo + lead, rows), (0, 0), (0, 0)))
        taken = lax.dynamic_slice_in_dim(padded, slab * zs, rows, 0)
        line = jnp.arange(rows)[:, None, None]
        taken = jnp.where(jnp.logical_and(line >= lead, line < lead + plan.z(halo)), taken, 0)
        return taken.reshape(rows, count * ys)

    wide = plan.x(halo)
    u_first = planes(0, wide, halo, plan.lead_in, plan.rows_in)
    c_last = planes(wide, plan.x(plan.halo_last), plan.halo_last, plan.lead_last, plan.rows_last)
    new_image, em_grad, packed = network(
        plan,
        grid,
        slab * zs,
        sector * xs,
        u_first,
        c_last,
        em_own.reshape(zs, xs * ys),
        cotangent.reshape(zs, xs * ys),
        weights,
    )
    cells = grid[0] * grid[1] * ys
    packed = lax.psum(packed, ("sector", "slab")) * (1.0 / math.sqrt(cells))
    grad_in, grad_mid, grad_out = unpack_grads(plan, packed)
    return (
        new_image.reshape(zs, xs, ys),
        em_grad.reshape(zs, xs, ys),
        grad_in,
        grad_mid,
        grad_out,
    )


def solution(mesh):
    placed = (
        P("slab", "sector", None),
        P("slab", "sector", None),
        P("sector", "slab", None, None),
        P("sector", "slab"),
        P("sector", "slab"),
        P("sector", "slab"),
        P("sector", None, None),
        P("sector", None, None),
        P(),
        P(),
        P(),
        P("slab", "sector", None),
    )
    return jax.shard_map(
        shards,
        mesh=mesh,
        in_specs=placed,
        out_specs=(P("slab", "sector", None), P("slab", "sector", None), P(), P(), P()),
        check_vma=False,
    )
```

```python
import math

import jax
import jax.numpy as jnp
from jax import lax
from jax.experimental import pallas as pl
from jax.experimental.pallas import tpu as pltpu
from jax.sharding import PartitionSpec as P

LANES = 128
VMEM_BYTES = 56 * 1024 * 1024


class Plan:
    def __init__(self, zs, xs, channels, layers):
        self.zs, self.xs, self.c, self.layers = zs, xs, channels, layers
        self.halo_u = [2 * layers - l + 1 for l in range(1, layers + 2)]
        self.halo_c = [l for l in range(1, layers + 1)]
        self.halo_in = 2 * layers
        self.halo_last = layers + 1
        self.lead_in = -(self.halo_in - 1) % 8
        self.lead_last = -(self.halo_last - 1) % 8
        self.rows_in = -(-(zs + 2 * self.halo_in + self.lead_in) // 8) * 8
        self.rows_last = -(-(zs + 2 * self.halo_last + self.lead_last) // 8) * 8

    def z(self, halo):
        return self.zs + 2 * halo

    def x(self, halo):
        return self.xs + 2 * halo

    def starts(self, planes):
        count = -(-planes // 6)
        size = -(-planes // count)
        return size, [min(k * size, planes - size) for k in range(count)]


def round_up(value, step):
    return -(-value // step) * step


def shifts(rows):
    lane = lax.broadcasted_iota(jnp.int32, rows.shape, 1)
    low = jnp.where(lane == 0, 0.0, pltpu.roll(rows, 1, 1))
    high = jnp.where(lane == LANES - 1, 0.0, pltpu.roll(rows, LANES - 1, 1))
    return low, rows, high


def prepare_kernel(plan, base_in, base_last, base_out, base_back, *refs):
    mids = 2 * (plan.layers - 1)
    bases, outs = refs[:mids], refs[mids:]
    w_first, w_top, w_out, w_back = outs[:4]
    toeplitz = outs[4:]
    c = plan.c
    for base, out, step, planes in (
        (base_in, w_first, 1, plan.z(plan.halo_u[1])),
        (base_last, w_top, 1, plan.z(plan.halo_c[-1])),
    ):
        rows = base[...].astype(jnp.float32)
        for k in range(planes):
            moved = rows if k == 0 else pltpu.roll(rows, k * step, 1)
            out[k * c : (k + 1) * c, :] = moved.astype(jnp.bfloat16)
    for base, out in ((base_out, w_out), (base_back, w_back)):
        rows = base[...].astype(jnp.float32)
        line = lax.broadcasted_iota(jnp.int32, rows.shape, 0)
        total = jnp.where(line == 0, rows, 0.0)
        for k in range(1, plan.zs):
            total = total + jnp.where(line == k, pltpu.roll(rows, k * c, 1), 0.0)
        out[...] = total.astype(jnp.bfloat16)
    for base, out in zip(bases, toeplitz):
        rows = base[...].astype(jnp.float32)
        for k in range(out.shape[0] // c):
            moved = rows if k == 0 else pltpu.roll(rows, k * c, 1)
            out[k * c : (k + 1) * c, :] = moved.astype(jnp.bfloat16)


def inside(first, count, c, bound):
    line = lax.broadcasted_iota(jnp.int32, (count * c, 1), 0)
    plane = first + lax.shift_right_arithmetic(line, int(math.log2(c)))
    return jnp.logical_and(plane >= 0, plane < bound)


def network_kernel(plan, grid, pos, u_first, c_last, em_own, cot_own, w_first, w_top, w_out, w_back, *refs):
    layers, c, zs, xs = plan.layers, plan.c, plan.zs, plan.xs
    mids = layers - 1
    w_fwd, w_bwd = refs[:mids], refs[mids : 2 * mids]
    new_image, em_grad, grads = refs[2 * mids : 2 * mids + 3]
    scratch = refs[2 * mids + 3 :]
    first_sh, last_sh = scratch[:2]
    u_sh = scratch[2 : 2 + layers]
    pre = scratch[2 + layers : 2 + 2 * layers]
    c_sh = scratch[2 + 2 * layers : 2 + 3 * layers]
    z_first, x_first = pos[0], pos[1]
    f32, bf16 = jnp.float32, jnp.bfloat16

    for source, target, count in (
        (u_first, first_sh, plan.x(plan.halo_in)),
        (c_last, last_sh, plan.x(plan.halo_last)),
    ):
        for k in range(count):
            span = slice(k * LANES, (k + 1) * LANES)
            for dy, rows in enumerate(shifts(source[:, span].astype(f32))):
                target[dy, :, span] = rows

    def store_shifted(target, value, rows, lane, x_at, keep):
        for half in range(2):
            part = value[:, half * LANES : (half + 1) * LANES]
            good = jnp.logical_and(x_at + half >= 0, x_at + half < grid[1])
            part = jnp.where(jnp.logical_and(keep, good), part, 0.0)
            for dy, moved in enumerate(shifts(part)):
                target[dy, rows, pl.ds(lane + half * LANES, LANES)] = moved.astype(bf16)

    def one_channel(source, weight, lane):
        pieces = [
            source[dy, :, pl.ds(lane + dx * LANES, 2 * LANES)] for dx in range(3) for dy in range(3)
        ]
        stacked = jnp.concatenate(pieces, axis=0).astype(bf16)
        return jnp.dot(weight[:, : stacked.shape[0]], stacked, preferred_element_type=f32)

    def many_channels(source, weight, first_plane, planes, lane):
        rows = slice(first_plane * c, (first_plane + planes + 2) * c)
        pieces = [
            source[dy, rows, pl.ds(lane + dx * LANES, 2 * LANES)]
            for dx in range(3)
            for dy in range(3)
        ]
        stacked = jnp.concatenate(pieces, axis=0)
        return jnp.dot(weight[:, : stacked.shape[0]], stacked, preferred_element_type=f32)

    def forward_tail(value, layer, first_plane, planes, pair, lane):
        halo = plan.halo_u[layer]
        rows = slice(first_plane * c, (first_plane + planes) * c)
        pre[layer - 1][rows, pl.ds(lane, 2 * LANES)] = value
        act = value * jax.nn.sigmoid(value)
        keep = inside(z_first - halo + first_plane, planes, c, grid[0])
        store_shifted(u_sh[layer - 1], act, rows, lane, x_first - halo + 2 * pair, keep)

    def backward_tail(value, layer, first_plane, planes, pair, lane):
        halo, halo_pre = plan.halo_c[layer - 1], plan.halo_u[layer]
        rows = slice(first_plane * c, (first_plane + planes) * c)
        from_plane = first_plane + halo_pre - halo
        preact = pre[layer - 1][
            from_plane * c : (from_plane + planes) * c,
            pl.ds(lane + (halo_pre - halo) * LANES, 2 * LANES),
        ]
        sigma = jax.nn.sigmoid(preact)
        slope = sigma * (1.0 + preact * (1.0 - sigma))
        keep = inside(z_first - halo + first_plane, planes, c, grid[0])
        store_shifted(
            c_sh[layer - 1], slope * value, rows, lane, x_first - halo + 2 * pair, keep
        )

    def over_pairs(count, body):
        def step(pair, carry):
            body(pair, pl.multiple_of(pair * 2 * LANES, 2 * LANES))
            return carry

        lax.fori_loop(0, count, step, 0)

    halo = plan.halo_u[1]

    def first_layer(pair, lane):
        value = one_channel(first_sh, w_first, lane)
        forward_tail(value, 1, 0, plan.z(halo), pair, lane)

    over_pairs(plan.x(halo) // 2, first_layer)
    for layer in range(2, layers + 1):
        halo = plan.halo_u[layer]
        size, starts = plan.starts(plan.z(halo))
        for start in starts:

            def middle(pair, lane, layer=layer, size=size, start=start):
                value = many_channels(u_sh[layer - 2], w_fwd[layer - 2], start, size, lane)
                forward_tail(value, layer, start, size, pair, lane)

            over_pairs(plan.x(halo) // 2, middle)

    def own_taps(source, halo):
        rows = slice((halo - 1) * c, (halo + zs + 1) * c)
        pieces = [
            source[dy, rows, (halo - 1 + dx) * LANES : (halo - 1 + dx + xs) * LANES]
            for dx in range(3)
            for dy in range(3)
        ]
        return jnp.concatenate(pieces, axis=0)

    top = plan.halo_u[layers]
    taps = own_taps(u_sh[layers - 1], top)
    last = jnp.dot(w_out[:, : taps.shape[0]], taps, preferred_element_type=f32)
    new_image[...] = em_own[...] + last[:zs, :]

    halo = plan.halo_c[-1]

    def top_layer(pair, lane):
        value = one_channel(last_sh, w_top, lane)
        backward_tail(value, layers, 0, plan.z(halo), pair, lane)

    over_pairs(plan.x(halo) // 2, top_layer)
    for layer in range(layers - 1, 0, -1):
        halo = plan.halo_c[layer - 1]
        size, starts = plan.starts(plan.z(halo))
        for start in starts:

            def middle_back(pair, lane, layer=layer, size=size, start=start):
                value = many_channels(c_sh[layer], w_bwd[layer - 1], start, size, lane)
                backward_tail(value, layer, start, size, pair, lane)

            over_pairs(plan.x(halo) // 2, middle_back)
    taps = own_taps(c_sh[0], plan.halo_c[0])
    down = jnp.dot(w_back[:, : taps.shape[0]], taps, preferred_element_type=f32)
    em_grad[...] = cot_own[...] + down[:zs, :]

    def own_rows(source, halo, plane):
        return source[1, (halo + plane) * c : (halo + plane + 1) * c, halo * LANES : (halo + xs) * LANES]

    def against(cells, taps):
        return lax.dot_general(cells, taps, (((1,), (1,)), ((), ())), preferred_element_type=f32)

    block = round_up(27 * c, LANES) // LANES
    for layer in range(2, layers + 1):
        source, halo = u_sh[layer - 2], plan.halo_u[layer - 1]
        total = None
        for plane in range(zs):
            first = halo - 1 + plane
            pieces = [
                source[
                    dy,
                    (first + dz) * c : (first + dz + 1) * c,
                    (halo - 1 + dx) * LANES : (halo - 1 + dx + xs) * LANES,
                ]
                for dz in range(3)
                for dx in range(3)
                for dy in range(3)
            ]
            pieces.append(jnp.zeros((block * LANES - 27 * c, xs * LANES), bf16))
            cells = own_rows(c_sh[layer - 1], plan.halo_c[layer - 1], plane)
            term = against(cells, jnp.concatenate(pieces, axis=0))
            total = term if total is None else total + term
        for k in range(block):
            at = ((layer - 2) * block + k) * c
            grads[at : at + c, :] = total[:, k * LANES : (k + 1) * LANES]

    def thin(source, halo, lead, cells_of, at):
        row = lead + halo - 1
        pieces = [
            source[dy, row : row + 8, (halo - 1 + dx) * LANES : (halo - 1 + dx + xs) * LANES]
            for dx in range(3)
            for dy in range(3)
        ]
        pieces.append(jnp.zeros((LANES - 72, xs * LANES), f32))
        taps = jnp.concatenate(pieces, axis=0).astype(bf16)
        total = None
        for plane in range(zs):
            term = against(cells_of(plane), taps)
            if plane:
                term = pltpu.roll(term, LANES - plane, 1)
            total = term if total is None else total + term
        grads[at : at + c, :] = total

    thin(
        first_sh,
        plan.halo_in,
        plan.lead_in,
        lambda plane: own_rows(c_sh[0], plan.halo_c[0], plane),
        mids * block * c,
    )
    thin(
        last_sh,
        plan.halo_last,
        plan.lead_last,
        lambda plane: own_rows(u_sh[layers - 1], top, plane),
        (mids * block + 1) * c,
    )
    used = (mids * block + 2) * c
    if used < grads.shape[0]:
        grads[used:, :] = jnp.zeros((grads.shape[0] - used, LANES), f32)


def toeplitz_bases(plan, w_in, w_mid, w_out):
    c, layers = plan.c, plan.layers
    mids = w_mid.shape[0]

    def spread(weights, planes, lead=0):
        moved = jnp.transpose(weights, (0, 2, 3, 1, 4))
        moved = jnp.pad(moved, ((0, 0), (0, 0), (0, 0), (lead, planes - 3 - lead), (0, 0)))
        flat = moved.reshape(weights.shape[0], 9 * planes * weights.shape[4])
        return jnp.pad(flat, ((0, 0), (0, round_up(flat.shape[1], LANES) - flat.shape[1])))

    first = jnp.transpose(w_in, (0, 2, 3, 4, 1))
    base_in = spread(first, plan.rows_in, plan.lead_in)
    last_back = jnp.transpose(jnp.flip(w_out, (2, 3, 4)), (1, 2, 3, 4, 0))
    base_last = spread(last_back, plan.rows_last, plan.lead_last)
    out_fwd = jnp.transpose(w_out, (0, 2, 3, 4, 1))
    in_back = jnp.transpose(jnp.flip(w_in, (2, 3, 4)), (1, 2, 3, 4, 0))
    base_out = jnp.broadcast_to(spread(out_fwd, plan.zs + 2), (8, round_up(9 * (plan.zs + 2) * c, LANES)))
    base_back = jnp.broadcast_to(spread(in_back, plan.zs + 2), base_out.shape)
    bases, sizes = [], []
    forward = jnp.transpose(w_mid, (0, 1, 3, 4, 5, 2))
    backward = jnp.transpose(jnp.flip(w_mid, (3, 4, 5)), (0, 2, 3, 4, 5, 1))
    for k in range(mids):
        size, _ = plan.starts(plan.z(plan.halo_u[k + 2]))
        bases.append(spread(forward[k], size + 2))
        sizes.append(size)
    for k in range(mids):
        size, _ = plan.starts(plan.z(plan.halo_c[k]))
        bases.append(spread(backward[k], size + 2))
        sizes.append(size)
    return (base_in, base_last, base_out, base_back, *bases), sizes


def prepared_weights(plan, w_in, w_mid, w_out):
    bases, sizes = toeplitz_bases(plan, w_in, w_mid, w_out)
    c, bf16 = plan.c, jnp.bfloat16
    shapes = [
        (plan.z(plan.halo_u[1]) * c, bases[0].shape[1]),
        (plan.z(plan.halo_c[-1]) * c, bases[1].shape[1]),
        bases[2].shape,
        bases[3].shape,
    ]
    shapes += [(size * c, base.shape[1]) for size, base in zip(sizes, bases[4:])]
    vmem = pl.BlockSpec(memory_space=pltpu.VMEM)
    return pl.pallas_call(
        lambda *refs: prepare_kernel(plan, *refs),
        out_shape=[jax.ShapeDtypeStruct(shape, bf16) for shape in shapes],
        in_specs=[vmem] * len(bases),
        out_specs=[vmem] * len(shapes),
        compiler_params=pltpu.CompilerParams(vmem_limit_bytes=VMEM_BYTES),
        name="prepare_weights",
    )(*bases)


def network(plan, grid, z_first, x_first, u_first, c_last, em_own, cot_own, weights, packed_rows):
    layers, c = plan.layers, plan.c
    f32, bf16 = jnp.float32, jnp.bfloat16
    own = jax.ShapeDtypeStruct((plan.zs, plan.xs * LANES), f32)
    scratch = [
        pltpu.VMEM((3, plan.rows_in, plan.x(plan.halo_in) * LANES), f32),
        pltpu.VMEM((3, plan.rows_last, plan.x(plan.halo_last) * LANES), f32),
    ]

    def region(halo, lead=()):
        return (*lead, plan.z(halo) * c, plan.x(halo) * LANES)

    scratch += [pltpu.VMEM(region(plan.halo_u[l], (3,)), bf16) for l in range(1, layers + 1)]
    scratch += [pltpu.VMEM(region(plan.halo_u[l]), f32) for l in range(1, layers + 1)]
    scratch += [pltpu.VMEM(region(plan.halo_c[l - 1], (3,)), bf16) for l in range(1, layers + 1)]
    vmem = pl.BlockSpec(memory_space=pltpu.VMEM)
    position = jnp.stack([z_first, x_first]).astype(jnp.int32)
    operands = (position, u_first, c_last, em_own, cot_own, *weights)
    return pl.pallas_call(
        lambda *refs: network_kernel(plan, grid, *refs),
        out_shape=[own, own, jax.ShapeDtypeStruct((packed_rows, LANES), f32)],
        in_specs=[pl.BlockSpec(memory_space=pltpu.SMEM)] + [vmem] * (len(operands) - 1),
        out_specs=[vmem] * 3,
        scratch_shapes=scratch,
        compiler_params=pltpu.CompilerParams(vmem_limit_bytes=VMEM_BYTES),
        name="network",
    )(*operands)


def grad_rows(plan):
    return ((plan.layers - 1) * (round_up(27 * plan.c, LANES) // LANES) + 2) * plan.c


def unpack_grads(plan, packed):
    c, mids = plan.c, plan.layers - 1
    block = round_up(27 * c, LANES) // LANES
    per = LANES // c
    blocks = packed[: grad_rows(plan)].reshape(mids * block + 2, c, LANES)
    mid = blocks[: mids * block].reshape(mids, block, c, per, c)
    mid = jnp.transpose(mid, (0, 1, 3, 2, 4)).reshape(mids, block * per, c, c)[:, :27]
    mid = jnp.transpose(mid.reshape(mids, 3, 3, 3, c, c), (0, 4, 5, 1, 2, 3))
    thin = blocks[mids * block :, :, :72].reshape(2, c, 3, 3, 8)[..., :3]
    thin = jnp.transpose(thin, (0, 1, 4, 2, 3))
    grad_in = thin[0][:, None]
    grad_out = jnp.flip(thin[1], (1, 2, 3))[None]
    return grad_in, mid, grad_out


CORES = 2


def along_chips(axis):
    count = lax.axis_size(axis)
    return [list(range(core, count, CORES)) for core in range(CORES)]


def within_chip(axis):
    count = lax.axis_size(axis)
    return [list(range(first, first + CORES)) for first in range(0, count, CORES)]


def to_all(value, axis, groups=None):
    count = lax.axis_size(axis) if groups is None else len(groups[0])
    copies = jnp.broadcast_to(value[None], (count, *value.shape))
    return lax.all_to_all(copies, axis, 0, 0, tiled=True, axis_index_groups=groups)


def pair_gather(value):
    return lax.all_gather(value, "sector", axis_index_groups=within_chip("sector"))


def summed_everywhere(packed, slabs):
    chips = along_chips("sector")
    core = lax.rem(lax.axis_index("sector"), CORES)
    share = packed.shape[0] // slabs
    parts = packed.reshape(slabs, share, LANES)
    own = jnp.sum(lax.all_to_all(parts, "slab", 0, 0, tiled=True), axis=0)
    both = pair_gather(own)
    own = both[0] + both[1]
    half = lax.dynamic_slice_in_dim(own, core * (share // CORES), share // CORES, 0)
    half = jnp.sum(to_all(half, "sector", chips), axis=0)
    halves = to_all(half, "slab")
    return jnp.transpose(pair_gather(halves), (1, 0, 2, 3)).reshape(packed.shape)


def shards(
    image,
    sensitivity,
    tile_values,
    tile_rows,
    tile_cols,
    tile_count,
    measured,
    background,
    w_in,
    w_mid,
    w_out,
    cotangent,
):
    f32, bf16 = jnp.float32, jnp.bfloat16
    highest = lax.Precision.HIGHEST
    sectors, slabs = lax.axis_size("sector"), lax.axis_size("slab")
    sector, slab = lax.axis_index("sector"), lax.axis_index("slab")
    zs, xs, ys = image.shape
    block_len = xs * ys
    line_blocks, row_len = measured.shape[1:]
    slots = tile_rows.shape[1]
    plan = Plan(zs, xs, w_in.shape[0], w_mid.shape[0] + 1)
    grid = (zs * slabs, xs * sectors)

    weights = prepared_weights(plan, w_in, w_mid, w_out)

    cells = zs * xs
    sent = [image, sensitivity, cotangent]
    sent = jnp.concatenate([field.reshape(cells, ys) for field in sent], axis=0)
    cols_row = jnp.pad(tile_cols.astype(f32), ((0, round_up(3 * cells + 1, 8) - 3 * cells - 1), (0, ys - slots)))
    sent = jnp.concatenate([sent, cols_row], axis=0)
    from_chips = to_all(sent, "sector", along_chips("sector"))
    every_cols = from_chips[:, 3 * cells, :slots].reshape(-1)
    got = jnp.transpose(pair_gather(from_chips)[:, :, : 3 * cells], (2, 1, 0, 3))
    got = got.reshape(3, zs, xs, sectors, ys)
    got = jnp.transpose(got, (0, 1, 3, 2, 4)).reshape(3, zs, sectors * xs, ys)
    image_slab, sens_slab, cot_slab = got[0], got[1], got[2]

    values = tile_values[0]
    weight = (jnp.arange(slots) < tile_count[0, 0]).astype(f32) / block_len
    blocks = image_slab.astype(bf16).reshape(zs * sectors, block_len)
    forward = jnp.einsum("krv,kv->kr", values, blocks[tile_cols[0]], preferred_element_type=f32)
    forward = forward * weight[:, None]
    lined = jnp.concatenate([forward, tile_rows[0].astype(f32)[:, None]], axis=1)
    lined = jnp.pad(lined, ((0, 0), (0, LANES - row_len - 1)))
    every = to_all(lined, "slab").reshape(slabs * slots, LANES)
    every_rows = every[:, row_len]
    placing = (every_rows[None, :] == jnp.arange(line_blocks, dtype=f32)[:, None]).astype(f32)
    projection = jnp.dot(placing, every[:, :row_len], precision=highest)
    ratio = (measured[0] / (projection + background[0])).astype(bf16)

    backward = jnp.einsum("krv,kr->kv", values, ratio[tile_rows[0]], preferred_element_type=f32)
    backward = backward * weight[:, None]
    every_back = to_all(backward, "sector", along_chips("sector")).reshape(-1, block_len)
    halo = plan.halo_in
    reach = -(-halo // xs)
    core = lax.rem(sector, CORES)
    span = 2 * reach + CORES
    near = sector - core - reach + jnp.arange(span)
    wanted = (jnp.arange(zs)[:, None] * sectors + near[None, :]).astype(f32)
    good = jnp.logical_and(near >= 0, near < sectors)
    wanted = jnp.where(good[None, :], wanted, -1.0).reshape(-1)
    owning = (every_cols[None, :] == wanted[:, None]).astype(f32)
    of_core = jnp.dot(owning, every_back, precision=highest)
    of_cores = pair_gather(of_core)
    back = (of_cores[0] + of_cores[1]).reshape(zs, span * xs, ys)
    back = lax.dynamic_slice_in_dim(back, core * xs + reach * xs - halo, xs + 2 * halo, 1)

    def window(field, halo, fill):
        padded = jnp.pad(field, ((0, 0), (halo, halo), (0, 0)), constant_values=fill)
        return lax.dynamic_slice_in_dim(padded, sector * xs, xs + 2 * halo, 1)

    em = window(image_slab, halo, 0.0) * back / window(sens_slab, halo, 1.0)
    em_own = em[:, halo : halo + xs]

    cot_wide = window(cot_slab, plan.halo_last, 0.0).astype(bf16)
    both = jnp.concatenate([em.astype(bf16), cot_wide], axis=1)
    every_plane = to_all(both, "slab").reshape(zs * slabs, both.shape[1], ys)

    def planes(lo, count, halo, lead, rows):
        field = every_plane[:, lo : lo + count]
        padded = jnp.pad(field, ((halo + lead, rows), (0, 0), (0, 0)))
        taken = lax.dynamic_slice_in_dim(padded, slab * zs, rows, 0)
        line = jnp.arange(rows)[:, None, None]
        taken = jnp.where(jnp.logical_and(line >= lead, line < lead + plan.z(halo)), taken, 0)
        return taken.reshape(rows, count * ys)

    wide = plan.x(halo)
    u_first = planes(0, wide, halo, plan.lead_in, plan.rows_in)
    c_last = planes(wide, plan.x(plan.halo_last), plan.halo_last, plan.lead_last, plan.rows_last)
    new_image, em_grad, packed = network(
        plan,
        grid,
        slab * zs,
        sector * xs,
        u_first,
        c_last,
        em_own.reshape(zs, xs * ys),
        cotangent.reshape(zs, xs * ys),
        weights,
        round_up(grad_rows(plan), slabs * CORES * 8),
    )
    packed = summed_everywhere(packed, slabs) * (1.0 / math.sqrt(grid[0] * grid[1] * ys))
    grad_in, grad_mid, grad_out = unpack_grads(plan, packed)
    return (
        new_image.reshape(zs, xs, ys),
        em_grad.reshape(zs, xs, ys),
        grad_in,
        grad_mid,
        grad_out,
    )


def solution(mesh):
    placed = (
        P("slab", "sector", None),
        P("slab", "sector", None),
        P("sector", "slab", None, None),
        P("sector", "slab"),
        P("sector", "slab"),
        P("sector", "slab"),
        P("sector", None, None),
        P("sector", None, None),
        P(),
        P(),
        P(),
        P("slab", "sector", None),
    )
    return jax.shard_map(
        shards,
        mesh=mesh,
        in_specs=placed,
        out_specs=(P("slab", "sector", None), P("slab", "sector", None), P(), P(), P()),
        check_vma=False,
    )
```

```python
import math

import jax
import jax.numpy as jnp
from jax import lax
from jax.experimental import pallas as pl
from jax.experimental.pallas import tpu as pltpu
from jax.sharding import PartitionSpec as P

LANES = 128
VMEM_BYTES = 56 * 1024 * 1024


class Plan:
    def __init__(self, zs, xs, channels, layers):
        self.zs, self.xs, self.c, self.layers = zs, xs, channels, layers
        self.halo_u = [2 * layers - l + 1 for l in range(1, layers + 2)]
        self.halo_c = [l for l in range(1, layers + 1)]
        self.halo_in = 2 * layers
        self.halo_last = layers + 1
        self.lead_in = -(self.halo_in - 1) % 8
        self.lead_last = -(self.halo_last - 1) % 8
        self.rows_in = -(-(zs + 2 * self.halo_in + self.lead_in) // 8) * 8
        self.rows_last = -(-(zs + 2 * self.halo_last + self.lead_last) // 8) * 8

    def z(self, halo):
        return self.zs + 2 * halo

    def x(self, halo):
        return self.xs + 2 * halo

    def starts(self, planes):
        count = -(-planes // 4)
        size = -(-planes // count)
        return size, [min(k * size, planes - size) for k in range(count)]


def round_up(value, step):
    return -(-value // step) * step


def shifts(rows):
    lane = lax.broadcasted_iota(jnp.int32, rows.shape, 1)
    low = jnp.where(lane == 0, 0.0, pltpu.roll(rows, 1, 1))
    high = jnp.where(lane == LANES - 1, 0.0, pltpu.roll(rows, LANES - 1, 1))
    return low, rows, high


def prepare_kernel(plan, w_in, w_mid, w_out, *outs):
    w_first, w_top, w_last, w_back = outs[:4]
    toeplitz = outs[4:]
    c, zs, mids = plan.c, plan.zs, plan.layers - 1
    f32, bf16 = jnp.float32, jnp.bfloat16

    def rolled(rows, out, step, planes):
        for k in range(planes):
            moved = rows if k == 0 else pltpu.roll(rows, k * step, 1)
            out[k * c : (k + 1) * c, :] = moved.astype(bf16)

    for weights, out, rows, lead, planes, mirrored in (
        (w_in, w_first, plan.rows_in, plan.lead_in, plan.z(plan.halo_u[1]), False),
        (w_out, w_top, plan.rows_last, plan.lead_last, plan.z(plan.halo_c[-1]), True),
    ):
        tap = lax.broadcasted_iota(jnp.int32, (27, out.shape[1]), 0)
        tap = 26 - tap if mirrored else tap
        at = lax.rem(tap, 9) * rows + lead + lax.div(tap, 9)
        lane = lax.broadcasted_iota(jnp.int32, at.shape, 1)
        chosen = jnp.where(lane == at, 1.0, 0.0).astype(bf16)
        base = lax.dot_general(
            weights[...], chosen, (((0,), (0,)), ((), ())), preferred_element_type=f32
        )
        rolled(base, out, 1, planes)

    def spread(tile, planes, width):
        pieces = []
        for k in range(9):
            pieces += [tile(0, k), tile(1, k), tile(2, k)]
            lines = pieces[0].shape[0]
            pieces.append(jnp.zeros((lines, (planes - 3) * c), f32))
        rest = width - 9 * planes * c
        if rest:
            pieces.append(jnp.zeros((lines, rest), f32))
        return jnp.concatenate(pieces, axis=1)

    for weights, out, mirrored in ((w_out, w_last, False), (w_in, w_back, True)):
        lines = weights[...].astype(f32)

        def row(dz, k, lines=lines, mirrored=mirrored):
            tap = 26 - dz * 9 - k if mirrored else dz * 9 + k
            return lines[tap : tap + 1, :]

        rows = jnp.broadcast_to(spread(row, zs + 2, out.shape[1]), out.shape)
        line = lax.broadcasted_iota(jnp.int32, rows.shape, 0)
        total = jnp.where(line == 0, rows, 0.0)
        for k in range(1, zs):
            total = total + jnp.where(line == k, pltpu.roll(rows, k * c, 1), 0.0)
        out[...] = total.astype(bf16)

    for index, out in enumerate(toeplitz):
        first = (index % mids) * 27

        def tile(dz, k, first=first, mirrored=index >= mids):
            if mirrored:
                return w_mid[first + 26 - dz * 9 - k].astype(f32).T
            return w_mid[first + dz * 9 + k].astype(f32)

        size = out.shape[0] // c
        rolled(spread(tile, size + 2, out.shape[1]), out, c, size)


def inside(first, count, c, bound):
    line = lax.broadcasted_iota(jnp.int32, (count * c, 1), 0)
    plane = first + lax.shift_right_arithmetic(line, int(math.log2(c)))
    return jnp.logical_and(plane >= 0, plane < bound)


def network_kernel(plan, grid, pos, u_first, c_last, em_own, cot_own, w_first, w_top, w_out, w_back, *refs):
    layers, c, zs, xs = plan.layers, plan.c, plan.zs, plan.xs
    mids = layers - 1
    w_fwd, w_bwd = refs[:mids], refs[mids : 2 * mids]
    new_image, em_grad, grads = refs[2 * mids : 2 * mids + 3]
    scratch = refs[2 * mids + 3 :]
    first_sh, last_sh = scratch[:2]
    u_sh = scratch[2 : 2 + layers]
    pre = scratch[2 + layers : 2 + 2 * layers]
    c_sh = scratch[2 + 2 * layers : 2 + 3 * layers]
    z_first, x_first = pos[0], pos[1]
    f32, bf16 = jnp.float32, jnp.bfloat16

    for source, target, count in (
        (u_first, first_sh, plan.x(plan.halo_in)),
        (c_last, last_sh, plan.x(plan.halo_last)),
    ):
        for k in range(count):
            span = slice(k * LANES, (k + 1) * LANES)
            for dy, rows in enumerate(shifts(source[:, span].astype(f32))):
                target[dy, :, span] = rows

    def store_shifted(target, value, rows, lane, x_at, keep):
        for half in range(2):
            part = value[:, half * LANES : (half + 1) * LANES]
            good = jnp.logical_and(x_at + half >= 0, x_at + half < grid[1])
            part = jnp.where(jnp.logical_and(keep, good), part, 0.0)
            for dy, moved in enumerate(shifts(part)):
                target[dy, rows, lane + half * LANES : lane + (half + 1) * LANES] = moved.astype(bf16)

    def one_channel(source, weight, lane):
        pieces = [
            source[dy, :, lane + dx * LANES : lane + (dx + 2) * LANES] for dx in range(3) for dy in range(3)
        ]
        stacked = jnp.concatenate(pieces, axis=0).astype(bf16)
        return jnp.dot(weight[:, : stacked.shape[0]], stacked, preferred_element_type=f32)

    def many_channels(source, weight, first_plane, planes, lane):
        rows = slice(first_plane * c, (first_plane + planes + 2) * c)
        pieces = [
            source[dy, rows, lane + dx * LANES : lane + (dx + 2) * LANES]
            for dx in range(3)
            for dy in range(3)
        ]
        stacked = jnp.concatenate(pieces, axis=0)
        return jnp.dot(weight[:, : stacked.shape[0]], stacked, preferred_element_type=f32)

    def forward_tail(value, layer, first_plane, planes, pair, lane):
        halo = plan.halo_u[layer]
        rows = slice(first_plane * c, (first_plane + planes) * c)
        pre[layer - 1][rows, lane : lane + 2 * LANES] = value
        act = value * jax.nn.sigmoid(value)
        keep = inside(z_first - halo + first_plane, planes, c, grid[0])
        store_shifted(u_sh[layer - 1], act, rows, lane, x_first - halo + 2 * pair, keep)

    def backward_tail(value, layer, first_plane, planes, pair, lane):
        halo, halo_pre = plan.halo_c[layer - 1], plan.halo_u[layer]
        rows = slice(first_plane * c, (first_plane + planes) * c)
        from_plane = first_plane + halo_pre - halo
        preact = pre[layer - 1][
            from_plane * c : (from_plane + planes) * c,
            lane + (halo_pre - halo) * LANES : lane + (halo_pre - halo + 2) * LANES,
        ]
        sigma = jax.nn.sigmoid(preact)
        slope = sigma * (1.0 + preact * (1.0 - sigma))
        keep = inside(z_first - halo + first_plane, planes, c, grid[0])
        store_shifted(
            c_sh[layer - 1], slope * value, rows, lane, x_first - halo + 2 * pair, keep
        )

    def over_pairs(count, body):
        for pair in range(count):
            body(pair, pair * 2 * LANES)

    halo = plan.halo_u[1]

    def first_layer(pair, lane):
        value = one_channel(first_sh, w_first, lane)
        forward_tail(value, 1, 0, plan.z(halo), pair, lane)

    over_pairs(plan.x(halo) // 2, first_layer)
    for layer in range(2, layers + 1):
        halo = plan.halo_u[layer]
        size, starts = plan.starts(plan.z(halo))
        for start in starts:

            def middle(pair, lane, layer=layer, size=size, start=start):
                value = many_channels(u_sh[layer - 2], w_fwd[layer - 2], start, size, lane)
                forward_tail(value, layer, start, size, pair, lane)

            over_pairs(plan.x(halo) // 2, middle)

    def own_taps(source, halo):
        rows = slice((halo - 1) * c, (halo + zs + 1) * c)
        pieces = [
            source[dy, rows, (halo - 1 + dx) * LANES : (halo - 1 + dx + xs) * LANES]
            for dx in range(3)
            for dy in range(3)
        ]
        return jnp.concatenate(pieces, axis=0)

    top = plan.halo_u[layers]
    taps = own_taps(u_sh[layers - 1], top)
    last = jnp.dot(w_out[:, : taps.shape[0]], taps, preferred_element_type=f32)
    new_image[...] = em_own[...] + last[:zs, :]

    halo = plan.halo_c[-1]

    def top_layer(pair, lane):
        value = one_channel(last_sh, w_top, lane)
        backward_tail(value, layers, 0, plan.z(halo), pair, lane)

    over_pairs(plan.x(halo) // 2, top_layer)
    for layer in range(layers - 1, 0, -1):
        halo = plan.halo_c[layer - 1]
        size, starts = plan.starts(plan.z(halo))
        for start in starts:

            def middle_back(pair, lane, layer=layer, size=size, start=start):
                value = many_channels(c_sh[layer], w_bwd[layer - 1], start, size, lane)
                backward_tail(value, layer, start, size, pair, lane)

            over_pairs(plan.x(halo) // 2, middle_back)
    taps = own_taps(c_sh[0], plan.halo_c[0])
    down = jnp.dot(w_back[:, : taps.shape[0]], taps, preferred_element_type=f32)
    em_grad[...] = cot_own[...] + down[:zs, :]

    def own_rows(source, halo, plane):
        return source[1, (halo + plane) * c : (halo + plane + 1) * c, halo * LANES : (halo + xs) * LANES]

    def against(cells, taps):
        return lax.dot_general(cells, taps, (((1,), (1,)), ((), ())), preferred_element_type=f32)

    block = round_up(27 * c, LANES) // LANES
    for layer in range(2, layers + 1):
        source, halo = u_sh[layer - 2], plan.halo_u[layer - 1]
        total = None
        for plane in range(zs):
            first = halo - 1 + plane
            pieces = [
                source[
                    dy,
                    (first + dz) * c : (first + dz + 1) * c,
                    (halo - 1 + dx) * LANES : (halo - 1 + dx + xs) * LANES,
                ]
                for dz in range(3)
                for dx in range(3)
                for dy in range(3)
            ]
            pieces.append(jnp.zeros((block * LANES - 27 * c, xs * LANES), bf16))
            cells = own_rows(c_sh[layer - 1], plan.halo_c[layer - 1], plane)
            term = against(cells, jnp.concatenate(pieces, axis=0))
            total = term if total is None else total + term
        for k in range(block):
            at = ((layer - 2) * block + k) * c
            grads[at : at + c, :] = total[:, k * LANES : (k + 1) * LANES]

    def thin(source, halo, lead, cells_of, at):
        row = lead + halo - 1
        pieces = [
            source[dy, row : row + 8, (halo - 1 + dx) * LANES : (halo - 1 + dx + xs) * LANES]
            for dx in range(3)
            for dy in range(3)
        ]
        pieces.append(jnp.zeros((LANES - 72, xs * LANES), f32))
        taps = jnp.concatenate(pieces, axis=0).astype(bf16)
        total = None
        for plane in range(zs):
            term = against(cells_of(plane), taps)
            if plane:
                term = pltpu.roll(term, LANES - plane, 1)
            total = term if total is None else total + term
        grads[at : at + c, :] = total

    thin(
        first_sh,
        plan.halo_in,
        plan.lead_in,
        lambda plane: own_rows(c_sh[0], plan.halo_c[0], plane),
        mids * block * c,
    )
    thin(
        last_sh,
        plan.halo_last,
        plan.lead_last,
        lambda plane: own_rows(u_sh[layers - 1], top, plane),
        (mids * block + 1) * c,
    )
    used = (mids * block + 2) * c
    if used < grads.shape[0]:
        grads[used:, :] = jnp.zeros((grads.shape[0] - used, LANES), f32)


def prepared_weights(plan, w_in, w_mid, w_out):
    c, mids = plan.c, plan.layers - 1
    bf16 = jnp.bfloat16

    def banded(halo):
        size, _ = plan.starts(plan.z(halo))
        return (size * c, round_up(9 * (size + 2) * c, LANES))

    last = (8, round_up(9 * (plan.zs + 2) * c, LANES))
    shapes = [
        (plan.z(plan.halo_u[1]) * c, round_up(9 * plan.rows_in, LANES)),
        (plan.z(plan.halo_c[-1]) * c, round_up(9 * plan.rows_last, LANES)),
        last,
        last,
    ]
    shapes += [banded(plan.halo_u[k + 2]) for k in range(mids)]
    shapes += [banded(plan.halo_c[k]) for k in range(mids)]
    vmem = pl.BlockSpec(memory_space=pltpu.VMEM)
    return pl.pallas_call(
        lambda *refs: prepare_kernel(plan, *refs),
        out_shape=[jax.ShapeDtypeStruct(shape, bf16) for shape in shapes],
        in_specs=[vmem] * 3,
        out_specs=[vmem] * len(shapes),
        compiler_params=pltpu.CompilerParams(vmem_limit_bytes=VMEM_BYTES),
        name="prepare_weights",
    )(
        jnp.transpose(w_in, (2, 3, 4, 1, 0)).reshape(27, c),
        jnp.transpose(w_mid, (0, 3, 4, 5, 1, 2)).reshape(mids * 27, c, c),
        jnp.transpose(w_out, (2, 3, 4, 0, 1)).reshape(27, c),
    )


def network(plan, grid, z_first, x_first, u_first, c_last, em_own, cot_own, weights, packed_rows):
    layers, c = plan.layers, plan.c
    f32, bf16 = jnp.float32, jnp.bfloat16
    own = jax.ShapeDtypeStruct((plan.zs, plan.xs * LANES), f32)
    scratch = [
        pltpu.VMEM((3, plan.rows_in, plan.x(plan.halo_in) * LANES), f32),
        pltpu.VMEM((3, plan.rows_last, plan.x(plan.halo_last) * LANES), f32),
    ]

    def region(halo, lead=()):
        return (*lead, plan.z(halo) * c, plan.x(halo) * LANES)

    scratch += [pltpu.VMEM(region(plan.halo_u[l], (3,)), bf16) for l in range(1, layers + 1)]
    scratch += [pltpu.VMEM(region(plan.halo_u[l]), f32) for l in range(1, layers + 1)]
    scratch += [pltpu.VMEM(region(plan.halo_c[l - 1], (3,)), bf16) for l in range(1, layers + 1)]
    vmem = pl.BlockSpec(memory_space=pltpu.VMEM)
    position = jnp.stack([z_first, x_first]).astype(jnp.int32)
    operands = (position, u_first, c_last, em_own, cot_own, *weights)
    return pl.pallas_call(
        lambda *refs: network_kernel(plan, grid, *refs),
        out_shape=[own, own, jax.ShapeDtypeStruct((packed_rows, LANES), f32)],
        in_specs=[pl.BlockSpec(memory_space=pltpu.SMEM)] + [vmem] * (len(operands) - 1),
        out_specs=[vmem] * 3,
        scratch_shapes=scratch,
        compiler_params=pltpu.CompilerParams(vmem_limit_bytes=VMEM_BYTES),
        name="network",
    )(*operands)


def grad_rows(plan):
    return ((plan.layers - 1) * (round_up(27 * plan.c, LANES) // LANES) + 2) * plan.c


def unpack_kernel(plan, factor, halves, grad_in, grad_mid, grad_out):
    c, mids = plan.c, plan.layers - 1
    block, per, rows = round_up(27 * c, LANES) // LANES, LANES // c, halves.shape[2]

    def packed(first):
        pieces = []
        for at in range(first, first + c, 8):
            slab, inner = divmod(at, CORES * rows)
            core, row = divmod(inner, rows)
            pieces.append(halves[core, slab, row : row + 8, :])
        return jnp.concatenate(pieces, axis=0) * factor

    for layer in range(mids):
        for k in range(block):
            lanes = packed((layer * block + k) * c)
            for tap in range(min(per, 27 - k * per)):
                grad_mid[layer * 27 + k * per + tap] = lanes[:, tap * c : (tap + 1) * c]
    for index, out in enumerate((grad_in, grad_out)):
        taps = packed((mids * block + index) * c).T
        for dz in range(3):
            for k in range(9):
                tap = dz * 9 + k
                out[26 - tap if index else tap] = taps[k * 8 + dz : k * 8 + dz + 1, :]


def unpack_grads(plan, halves, factor):
    c, mids = plan.c, plan.layers - 1
    f32 = jnp.float32
    thin = jax.ShapeDtypeStruct((27, 1, c), f32)
    vmem = pl.BlockSpec(memory_space=pltpu.VMEM)
    grad_in, mid, grad_out = pl.pallas_call(
        lambda *refs: unpack_kernel(plan, factor, *refs),
        out_shape=[thin, jax.ShapeDtypeStruct((mids * 27, c, c), f32), thin],
        in_specs=[vmem],
        out_specs=[vmem] * 3,
        compiler_params=pltpu.CompilerParams(vmem_limit_bytes=VMEM_BYTES),
        name="unpack_gradients",
    )(halves)
    mid = jnp.transpose(mid.reshape(mids, 3, 3, 3, c, c), (0, 4, 5, 1, 2, 3))
    grad_in = jnp.transpose(grad_in.reshape(3, 3, 3, 1, c), (4, 3, 0, 1, 2))
    grad_out = jnp.transpose(grad_out.reshape(3, 3, 3, 1, c), (3, 4, 0, 1, 2))
    return grad_in, mid, grad_out


CORES = 2


def along_chips(axis):
    count = lax.axis_size(axis)
    return [list(range(core, count, CORES)) for core in range(CORES)]


def within_chip(axis):
    count = lax.axis_size(axis)
    return [list(range(first, first + CORES)) for first in range(0, count, CORES)]


def to_all(value, axis, groups=None):
    count = lax.axis_size(axis) if groups is None else len(groups[0])
    copies = jnp.broadcast_to(value[None], (count, *value.shape))
    return lax.all_to_all(copies, axis, 0, 0, tiled=True, axis_index_groups=groups)


def pair_gather(value):
    return lax.all_gather(value, "sector", axis_index_groups=within_chip("sector"))


def summed_everywhere(packed, slabs):
    chips = along_chips("sector")
    core = lax.rem(lax.axis_index("sector"), CORES)
    share = packed.shape[0] // slabs
    parts = packed.reshape(slabs, share, LANES)
    own = jnp.sum(lax.all_to_all(parts, "slab", 0, 0, tiled=True), axis=0)
    both = pair_gather(own)
    own = both[0] + both[1]
    half = lax.dynamic_slice_in_dim(own, core * (share // CORES), share // CORES, 0)
    half = to_all(half.astype(jnp.bfloat16), "sector", chips)
    half = jnp.sum(half.astype(jnp.float32), axis=0)
    return pair_gather(to_all(half, "slab"))


def shards(
    image,
    sensitivity,
    tile_values,
    tile_rows,
    tile_cols,
    tile_count,
    measured,
    background,
    w_in,
    w_mid,
    w_out,
    cotangent,
):
    f32, bf16 = jnp.float32, jnp.bfloat16
    highest = lax.Precision.HIGHEST
    sectors, slabs = lax.axis_size("sector"), lax.axis_size("slab")
    sector, slab = lax.axis_index("sector"), lax.axis_index("slab")
    zs, xs, ys = image.shape
    block_len = xs * ys
    line_blocks, row_len = measured.shape[1:]
    slots = tile_rows.shape[1]
    plan = Plan(zs, xs, w_in.shape[0], w_mid.shape[0] + 1)
    grid = (zs * slabs, xs * sectors)

    cells = zs * xs
    chips = along_chips("sector")
    cols_row = jnp.pad(tile_cols.astype(bf16), ((0, round_up(cells + 1, 8) - cells - 1), (0, ys - slots)))
    sent = jnp.concatenate([image.astype(bf16).reshape(cells, ys), cols_row], axis=0)
    from_chips = to_all(sent, "sector", chips)
    every_cols = from_chips[:, cells, :slots].astype(f32).reshape(-1)
    got = pair_gather(from_chips[:, :cells])
    got = jnp.transpose(got.reshape(CORES, len(chips[0]), zs, xs, ys), (2, 1, 0, 3, 4))
    blocks = got.reshape(zs * sectors, block_len)

    fields = jnp.concatenate([field.reshape(cells, ys) for field in (image, sensitivity, cotangent)], axis=0)
    fields = jnp.pad(fields, ((0, round_up(3 * cells, 8) - 3 * cells), (0, 0)))
    fields, from_chips = lax.optimization_barrier((fields, from_chips))
    reach = -(-plan.halo_in // (xs * CORES))
    near_fields = []
    for chip in range(-reach, reach + 1):
        step = chip * CORES
        pairs = [(k + step, k) for k in range(sectors) if 0 <= k + step < sectors]
        near_fields.append(lax.ppermute(fields, "sector", pairs) if chip else fields)
    near_fields = jnp.concatenate([field[: 3 * cells] for field in near_fields], axis=0)

    values = tile_values[0]
    weight = (jnp.arange(slots) < tile_count[0, 0]).astype(f32) / block_len
    forward = jnp.einsum("krv,kv->kr", values, blocks[tile_cols[0]], preferred_element_type=f32)
    forward = forward * weight[:, None]
    lined = jnp.concatenate([forward, tile_rows[0].astype(f32)[:, None]], axis=1)
    lined = jnp.pad(lined, ((0, 0), (0, LANES - row_len - 1)))
    every = to_all(lined, "slab").reshape(slabs * slots, LANES)
    every_rows = every[:, row_len]
    placing = (every_rows[None, :] == jnp.arange(line_blocks, dtype=f32)[:, None]).astype(f32)
    projection = jnp.dot(placing, every[:, :row_len], precision=highest)
    ratio = (measured[0] / (projection + background[0])).astype(bf16)

    backward = jnp.einsum("krv,kr->kv", values, ratio[tile_rows[0]], preferred_element_type=f32)
    backward = backward * weight[:, None]
    every_back = to_all(backward, "sector", chips).reshape(-1, block_len)
    weights = prepared_weights(plan, w_in, w_mid, w_out)
    every_back, weights = lax.optimization_barrier((every_back, weights))
    halo = plan.halo_in
    core = lax.rem(sector, CORES)
    span = (2 * reach + 1) * CORES
    near = sector - core - reach * CORES + jnp.arange(span)
    wanted = (jnp.arange(zs)[:, None] * sectors + near[None, :]).astype(f32)
    good = jnp.logical_and(near >= 0, near < sectors)
    wanted = jnp.where(good[None, :], wanted, -1.0).reshape(-1)
    owning = (every_cols[None, :] == wanted[:, None]).astype(f32)
    of_core = jnp.dot(owning, every_back, precision=highest).reshape(-1, ys)
    of_cores = pair_gather(jnp.concatenate([of_core, near_fields], axis=0))
    back = of_cores[:, : of_core.shape[0]]
    back = (back[0] + back[1]).reshape(zs, span * xs, ys)
    near_fields = of_cores[:, of_core.shape[0] :].reshape(CORES, 2 * reach + 1, 3, zs, xs, ys)
    near_fields = jnp.transpose(near_fields, (2, 3, 1, 0, 4, 5)).reshape(3, zs, span * xs, ys)
    row = (sector - core - reach * CORES) * xs + jnp.arange(span * xs)
    good = jnp.logical_and(row >= 0, row < grid[1])[None, :, None]
    em = jnp.where(good, near_fields[0] * back / near_fields[1], 0.0)
    cot_near = jnp.where(good, near_fields[2], 0.0)

    def window(field, halo):
        return lax.dynamic_slice_in_dim(field, (core + reach * CORES) * xs - halo, xs + 2 * halo, 1)

    em_own = window(em, 0)

    both = [window(em, halo).astype(bf16), window(cot_near, plan.halo_last).astype(bf16)]
    both = jnp.concatenate(both, axis=1)
    every_plane = to_all(both, "slab").reshape(zs * slabs, both.shape[1], ys)

    def planes(lo, count, halo, lead, rows):
        field = every_plane[:, lo : lo + count]
        padded = jnp.pad(field, ((halo + lead, rows), (0, 0), (0, 0)))
        taken = lax.dynamic_slice_in_dim(padded, slab * zs, rows, 0)
        line = jnp.arange(rows)[:, None, None]
        taken = jnp.where(jnp.logical_and(line >= lead, line < lead + plan.z(halo)), taken, 0)
        return taken.reshape(rows, count * ys)

    wide = plan.x(halo)
    u_first = planes(0, wide, halo, plan.lead_in, plan.rows_in)
    c_last = planes(wide, plan.x(plan.halo_last), plan.halo_last, plan.lead_last, plan.rows_last)
    new_image, em_grad, packed = network(
        plan,
        grid,
        slab * zs,
        sector * xs,
        u_first,
        c_last,
        em_own.reshape(zs, xs * ys),
        cotangent.reshape(zs, xs * ys),
        weights,
        round_up(grad_rows(plan), slabs * CORES * 8),
    )
    halves = summed_everywhere(packed, slabs)
    factor = 1.0 / math.sqrt(grid[0] * grid[1] * ys)
    grad_in, grad_mid, grad_out = unpack_grads(plan, halves, factor)
    return (
        new_image.reshape(zs, xs, ys),
        em_grad.reshape(zs, xs, ys),
        grad_in,
        grad_mid,
        grad_out,
    )


def solution(mesh):
    placed = (
        P("slab", "sector", None),
        P("slab", "sector", None),
        P("sector", "slab", None, None),
        P("sector", "slab"),
        P("sector", "slab"),
        P("sector", "slab"),
        P("sector", None, None),
        P("sector", None, None),
        P(),
        P(),
        P(),
        P("slab", "sector", None),
    )
    return jax.shard_map(
        shards,
        mesh=mesh,
        in_specs=placed,
        out_specs=(P("slab", "sector", None), P("slab", "sector", None), P(), P(), P()),
        check_vma=False,
    )
```

```python
import math

import jax
import jax.numpy as jnp
from jax import lax
from jax.experimental import pallas as pl
from jax.experimental.pallas import tpu as pltpu
from jax.sharding import PartitionSpec as P

LANES = 128
VMEM_BYTES = 56 * 1024 * 1024


class Plan:
    def __init__(self, zs, xs, channels, layers):
        self.zs, self.xs, self.c, self.layers = zs, xs, channels, layers
        self.halo_u = [2 * layers - l + 1 for l in range(1, layers + 2)]
        self.halo_c = [l for l in range(1, layers + 1)]
        self.halo_in = 2 * layers
        self.halo_last = layers + 1
        self.lead_in = -(self.halo_in - 1) % 8
        self.lead_last = -(self.halo_last - 1) % 8
        self.rows_in = -(-(zs + 2 * self.halo_in + self.lead_in) // 8) * 8
        self.rows_last = -(-(zs + 2 * self.halo_last + self.lead_last) // 8) * 8

    def z(self, halo):
        return self.zs + 2 * halo

    def x(self, halo):
        return self.xs + 2 * halo

    def starts(self, planes):
        count = -(-planes // 2)
        size = -(-planes // count)
        return size, [min(k * size, planes - size) for k in range(count)]


def round_up(value, step):
    return -(-value // step) * step


def shifts(rows):
    lane = lax.broadcasted_iota(jnp.int32, rows.shape, 1)
    low = jnp.where(lane == 0, 0.0, pltpu.roll(rows, 1, 1))
    high = jnp.where(lane == LANES - 1, 0.0, pltpu.roll(rows, LANES - 1, 1))
    return low, rows, high


def prepare_kernel(plan, w_in, w_mid, w_out, *outs):
    w_first, w_top, w_last, w_back = outs[:4]
    toeplitz = outs[4:]
    c, zs, mids = plan.c, plan.zs, plan.layers - 1
    f32, bf16 = jnp.float32, jnp.bfloat16

    def rolled(rows, out, step, planes, first=0):
        for k in range(planes):
            moved = rows if k == 0 else pltpu.roll(rows, k * step, 1)
            out[(first + k) * c : (first + k + 1) * c, :] = moved.astype(bf16)

    for weights, out, rows, lead, planes, mirrored in (
        (w_in, w_first, plan.rows_in, plan.lead_in, plan.z(plan.halo_u[1]), False),
        (w_out, w_top, plan.rows_last, plan.lead_last, plan.z(plan.halo_c[-1]), True),
    ):
        tap = lax.broadcasted_iota(jnp.int32, (27, out.shape[1]), 0)
        tap = 26 - tap if mirrored else tap
        at = lax.rem(tap, 9) * rows + lead + lax.div(tap, 9)
        lane = lax.broadcasted_iota(jnp.int32, at.shape, 1)
        chosen = jnp.where(lane == at, 1.0, 0.0).astype(bf16)
        base = lax.dot_general(
            weights[...], chosen, (((0,), (0,)), ((), ())), preferred_element_type=f32
        )
        rolled(base, out, 1, planes)

    def spread(tile, taps, planes, width):
        pieces = []
        for k in taps:
            pieces += [tile(0, k), tile(1, k), tile(2, k)]
            lines = pieces[0].shape[0]
            pieces.append(jnp.zeros((lines, (planes - 3) * c), f32))
        rest = width - len(taps) * planes * c
        if rest:
            pieces.append(jnp.zeros((lines, rest), f32))
        return jnp.concatenate(pieces, axis=1)

    for weights, out, mirrored in ((w_out, w_last, False), (w_in, w_back, True)):
        lines = weights[...].astype(f32)

        def row(dz, k, lines=lines, mirrored=mirrored):
            tap = 26 - dz * 9 - k if mirrored else dz * 9 + k
            return lines[tap : tap + 1, :]

        rows = jnp.broadcast_to(spread(row, range(9), zs + 2, out.shape[1]), out.shape)
        line = lax.broadcasted_iota(jnp.int32, rows.shape, 0)
        total = jnp.where(line == 0, rows, 0.0)
        for k in range(1, zs):
            total = total + jnp.where(line == k, pltpu.roll(rows, k * c, 1), 0.0)
        out[...] = total.astype(bf16)

    for index, out in enumerate(toeplitz):
        first = (index % mids) * 27

        def tile(dz, k, first=first, mirrored=index >= mids):
            if mirrored:
                return w_mid[first + 26 - dz * 9 - k].astype(f32).T
            return w_mid[first + dz * 9 + k].astype(f32)

        size = out.shape[0] // (3 * c)
        for dx in range(3):
            rows = spread(tile, range(dx * 3, dx * 3 + 3), size + 2, out.shape[1])
            rolled(rows, out, c, size, dx * size)


def inside(first, count, c, bound):
    line = lax.broadcasted_iota(jnp.int32, (count * c, 1), 0)
    plane = first + lax.shift_right_arithmetic(line, int(math.log2(c)))
    return jnp.logical_and(plane >= 0, plane < bound)


def network_kernel(plan, grid, pos, received, em_own, cot_own, w_first, w_top, w_out, w_back, *refs):
    layers, c, zs, xs = plan.layers, plan.c, plan.zs, plan.xs
    mids = layers - 1
    w_fwd, w_bwd = refs[:mids], refs[mids : 2 * mids]
    new_image, em_grad, grads = refs[2 * mids : 2 * mids + 3]
    scratch = refs[2 * mids + 3 :]
    first_sh, last_sh = scratch[:2]
    u_sh = scratch[2 : 2 + layers]
    pre = scratch[2 + layers : 2 + 2 * layers]
    c_sh = scratch[2 + 2 * layers : 2 + 3 * layers]
    z_first, x_first = pos[0], pos[1]
    f32, bf16 = jnp.float32, jnp.bfloat16

    wide = plan.x(plan.halo_in)
    for target, gathered, halo, lead, first_row in (
        (first_sh, scratch[-2], plan.halo_in, plan.lead_in, 0),
        (last_sh, scratch[-1], plan.halo_last, plan.lead_last, wide),
    ):
        gathered[...] = jnp.zeros(gathered.shape, f32)
        for k in range(plan.z(halo)):
            plane = z_first - halo + k
            inner = jnp.logical_and(plane >= 0, plane < grid[0])
            rows = received[jnp.clip(plane, 0, grid[0] - 1)].astype(f32)
            rows = jnp.where(inner, rows, 0.0)
            for x in range(plan.x(halo)):
                span = slice(x * LANES, (x + 1) * LANES)
                gathered[lead + k : lead + k + 1, span] = rows[first_row + x : first_row + x + 1, :]
        for x in range(plan.x(halo)):
            span = slice(x * LANES, (x + 1) * LANES)
            for dy, rows in enumerate(shifts(gathered[:, span])):
                target[dy, :, span] = rows

    def store_shifted(target, value, rows, lane, x_at, keep):
        for half in range(2):
            part = value[:, half * LANES : (half + 1) * LANES]
            good = jnp.logical_and(x_at + half >= 0, x_at + half < grid[1])
            part = jnp.where(jnp.logical_and(keep, good), part, 0.0)
            for dy, moved in enumerate(shifts(part)):
                target[dy, rows, lane + half * LANES : lane + (half + 1) * LANES] = moved.astype(bf16)

    def one_channel(source, weight, lane):
        pieces = [
            source[dy, :, lane + dx * LANES : lane + (dx + 2) * LANES] for dx in range(3) for dy in range(3)
        ]
        stacked = jnp.concatenate(pieces, axis=0).astype(bf16)
        return jnp.dot(weight[:, : stacked.shape[0]], stacked, preferred_element_type=f32)

    def many_channels(source, weight, first_plane, planes, count):
        rows = slice(first_plane * c, (first_plane + planes + 2) * c)
        lines = planes * c

        def product(pair):
            span = slice(pair * 2 * LANES, (pair + 1) * 2 * LANES)
            stacked = jnp.concatenate([source[dy, rows, span] for dy in range(3)], axis=0)
            return jnp.dot(weight[:, : stacked.shape[0]], stacked, preferred_element_type=f32)

        left = product(0)
        for pair in range(count):
            right = product(pair + 1)
            middle = [left[lines : 2 * lines, LANES:], right[lines : 2 * lines, :LANES]]
            yield left[:lines] + jnp.concatenate(middle, axis=1) + right[2 * lines :]
            left = right

    def forward_tail(value, layer, first_plane, planes, pair, lane):
        halo = plan.halo_u[layer]
        rows = slice(first_plane * c, (first_plane + planes) * c)
        pre[layer - 1][rows, lane : lane + 2 * LANES] = value
        act = value * jax.nn.sigmoid(value)
        keep = inside(z_first - halo + first_plane, planes, c, grid[0])
        store_shifted(u_sh[layer - 1], act, rows, lane, x_first - halo + 2 * pair, keep)

    def backward_tail(value, layer, first_plane, planes, pair, lane):
        halo, halo_pre = plan.halo_c[layer - 1], plan.halo_u[layer]
        rows = slice(first_plane * c, (first_plane + planes) * c)
        from_plane = first_plane + halo_pre - halo
        preact = pre[layer - 1][
            from_plane * c : (from_plane + planes) * c,
            lane + (halo_pre - halo) * LANES : lane + (halo_pre - halo + 2) * LANES,
        ]
        sigma = jax.nn.sigmoid(preact)
        slope = sigma * (1.0 + preact * (1.0 - sigma))
        keep = inside(z_first - halo + first_plane, planes, c, grid[0])
        store_shifted(
            c_sh[layer - 1], slope * value, rows, lane, x_first - halo + 2 * pair, keep
        )

    halo = plan.halo_u[1]
    for pair in range(plan.x(halo) // 2):
        lane = pair * 2 * LANES
        forward_tail(one_channel(first_sh, w_first, lane), 1, 0, plan.z(halo), pair, lane)
    for layer in range(2, layers + 1):
        halo = plan.halo_u[layer]
        size, starts = plan.starts(plan.z(halo))
        for start in starts:
            values = many_channels(
                u_sh[layer - 2], w_fwd[layer - 2], start, size, plan.x(halo) // 2
            )
            for pair, value in enumerate(values):
                forward_tail(value, layer, start, size, pair, pair * 2 * LANES)

    def own_taps(source, halo):
        rows = slice((halo - 1) * c, (halo + zs + 1) * c)
        pieces = [
            source[dy, rows, (halo - 1 + dx) * LANES : (halo - 1 + dx + xs) * LANES]
            for dx in range(3)
            for dy in range(3)
        ]
        return jnp.concatenate(pieces, axis=0)

    top = plan.halo_u[layers]
    taps = own_taps(u_sh[layers - 1], top)
    last = jnp.dot(w_out[:, : taps.shape[0]], taps, preferred_element_type=f32)
    new_image[...] = em_own[...] + last[:zs, :]

    halo = plan.halo_c[-1]

    for pair in range(plan.x(halo) // 2):
        lane = pair * 2 * LANES
        backward_tail(one_channel(last_sh, w_top, lane), layers, 0, plan.z(halo), pair, lane)
    for layer in range(layers - 1, 0, -1):
        halo = plan.halo_c[layer - 1]
        size, starts = plan.starts(plan.z(halo))
        for start in starts:
            values = many_channels(c_sh[layer], w_bwd[layer - 1], start, size, plan.x(halo) // 2)
            for pair, value in enumerate(values):
                backward_tail(value, layer, start, size, pair, pair * 2 * LANES)
    taps = own_taps(c_sh[0], plan.halo_c[0])
    down = jnp.dot(w_back[:, : taps.shape[0]], taps, preferred_element_type=f32)
    em_grad[...] = cot_own[...] + down[:zs, :]

    def own_rows(source, halo, plane):
        return source[1, (halo + plane) * c : (halo + plane + 1) * c, halo * LANES : (halo + xs) * LANES]

    def against(cells, taps):
        return lax.dot_general(cells, taps, (((1,), (1,)), ((), ())), preferred_element_type=f32)

    block = round_up(27 * c, LANES) // LANES
    for layer in range(2, layers + 1):
        source, halo = u_sh[layer - 2], plan.halo_u[layer - 1]
        total = None
        for plane in range(zs):
            first = halo - 1 + plane
            pieces = [
                source[
                    dy,
                    (first + dz) * c : (first + dz + 1) * c,
                    (halo - 1 + dx) * LANES : (halo - 1 + dx + xs) * LANES,
                ]
                for dz in range(3)
                for dx in range(3)
                for dy in range(3)
            ]
            pieces.append(jnp.zeros((block * LANES - 27 * c, xs * LANES), bf16))
            cells = own_rows(c_sh[layer - 1], plan.halo_c[layer - 1], plane)
            term = against(cells, jnp.concatenate(pieces, axis=0))
            total = term if total is None else total + term
        for k in range(block):
            at = ((layer - 2) * block + k) * c
            grads[at : at + c, :] = total[:, k * LANES : (k + 1) * LANES]

    def thin(source, halo, lead, cells_of, at):
        row = lead + halo - 1
        pieces = [
            source[dy, row : row + 8, (halo - 1 + dx) * LANES : (halo - 1 + dx + xs) * LANES]
            for dx in range(3)
            for dy in range(3)
        ]
        pieces.append(jnp.zeros((LANES - 72, xs * LANES), f32))
        taps = jnp.concatenate(pieces, axis=0).astype(bf16)
        total = None
        for plane in range(zs):
            term = against(cells_of(plane), taps)
            if plane:
                term = pltpu.roll(term, LANES - plane, 1)
            total = term if total is None else total + term
        grads[at : at + c, :] = total

    thin(
        first_sh,
        plan.halo_in,
        plan.lead_in,
        lambda plane: own_rows(c_sh[0], plan.halo_c[0], plane),
        mids * block * c,
    )
    thin(
        last_sh,
        plan.halo_last,
        plan.lead_last,
        lambda plane: own_rows(u_sh[layers - 1], top, plane),
        (mids * block + 1) * c,
    )
    used = (mids * block + 2) * c
    if used < grads.shape[0]:
        grads[used:, :] = jnp.zeros((grads.shape[0] - used, LANES), f32)


def prepared_weights(plan, w_in, w_mid, w_out):
    c, mids = plan.c, plan.layers - 1
    bf16 = jnp.bfloat16

    def banded(halo):
        size, _ = plan.starts(plan.z(halo))
        return (3 * size * c, round_up(3 * (size + 2) * c, LANES))

    last = (8, round_up(9 * (plan.zs + 2) * c, LANES))
    shapes = [
        (plan.z(plan.halo_u[1]) * c, round_up(9 * plan.rows_in, LANES)),
        (plan.z(plan.halo_c[-1]) * c, round_up(9 * plan.rows_last, LANES)),
        last,
        last,
    ]
    shapes += [banded(plan.halo_u[k + 2]) for k in range(mids)]
    shapes += [banded(plan.halo_c[k]) for k in range(mids)]
    vmem = pl.BlockSpec(memory_space=pltpu.VMEM)
    return pl.pallas_call(
        lambda *refs: prepare_kernel(plan, *refs),
        out_shape=[jax.ShapeDtypeStruct(shape, bf16) for shape in shapes],
        in_specs=[vmem] * 3,
        out_specs=[vmem] * len(shapes),
        compiler_params=pltpu.CompilerParams(vmem_limit_bytes=VMEM_BYTES),
        name="prepare_weights",
    )(
        jnp.transpose(w_in, (2, 3, 4, 1, 0)).reshape(27, c),
        jnp.transpose(w_mid, (0, 3, 4, 5, 1, 2)).reshape(mids * 27, c, c),
        jnp.transpose(w_out, (2, 3, 4, 0, 1)).reshape(27, c),
    )


def network(plan, grid, position, received, em_own, cot_own, weights, packed_rows):
    layers, c = plan.layers, plan.c
    f32, bf16 = jnp.float32, jnp.bfloat16
    own = jax.ShapeDtypeStruct((plan.zs, plan.xs * LANES), f32)
    scratch = [
        pltpu.VMEM((3, plan.rows_in, plan.x(plan.halo_in) * LANES), f32),
        pltpu.VMEM((3, plan.rows_last, plan.x(plan.halo_last) * LANES), f32),
    ]

    def region(halo, lead=()):
        return (*lead, plan.z(halo) * c, plan.x(halo) * LANES)

    scratch += [pltpu.VMEM(region(plan.halo_u[l], (3,)), bf16) for l in range(1, layers + 1)]
    scratch += [pltpu.VMEM(region(plan.halo_u[l]), f32) for l in range(1, layers + 1)]
    scratch += [pltpu.VMEM(region(plan.halo_c[l - 1], (3,)), bf16) for l in range(1, layers + 1)]
    vmem = pl.BlockSpec(memory_space=pltpu.VMEM)
    scratch += [
        pltpu.VMEM((plan.rows_in, plan.x(plan.halo_in) * LANES), f32),
        pltpu.VMEM((plan.rows_last, plan.x(plan.halo_last) * LANES), f32),
    ]
    operands = (position, received, em_own, cot_own, *weights)
    return pl.pallas_call(
        lambda *refs: network_kernel(plan, grid, *refs),
        out_shape=[own, own, jax.ShapeDtypeStruct((packed_rows, LANES), f32)],
        in_specs=[pl.BlockSpec(memory_space=pltpu.SMEM)] + [vmem] * (len(operands) - 1),
        out_specs=[vmem] * 3,
        scratch_shapes=scratch,
        compiler_params=pltpu.CompilerParams(vmem_limit_bytes=VMEM_BYTES),
        name="network",
    )(*operands)


def image_kernel(plan, grid, copies, pos, parts, sent, em_own, cot_own):
    zs, xs, halo, outer = plan.zs, plan.xs, plan.halo_in, plan.halo_last
    reach = -(-halo // (xs * CORES))
    span = (2 * reach + 1) * CORES * xs
    x_first = pos[1]
    core = lax.rem(lax.div(x_first, xs), CORES)
    row = x_first - (core + reach * CORES) * xs + lax.broadcasted_iota(jnp.int32, (span, LANES), 0)
    good = jnp.logical_and(row >= 0, row < grid[1])

    def near(field, z):
        pieces = []
        for chip in range(2 * reach + 1):
            at = zs * span + (chip * 3 + field) * zs * xs + z * xs
            pieces += [parts[k, at : at + xs, :] for k in range(CORES)]
        return jnp.concatenate(pieces, axis=0)

    def window(rows, halo):
        first = reach * CORES * xs - halo
        count = xs + 2 * halo
        taken = rows[first : first + count]
        for k in range(1, CORES):
            taken = jnp.where(core == k, rows[first + k * xs : first + k * xs + count], taken)
        return taken

    for z in range(zs):
        back = parts[0, z * span : (z + 1) * span, :]
        for k in range(1, CORES):
            back = back + parts[k, z * span : (z + 1) * span, :]
        em = window(jnp.where(good, near(0, z) * back / near(1, z), 0.0), halo)
        cot = window(jnp.where(good, near(2, z), 0.0), outer)
        both = jnp.concatenate([em, cot], axis=0).astype(jnp.bfloat16)
        for k in range(copies):
            sent[k, z] = both
        for x in range(xs):
            lanes = slice(x * LANES, (x + 1) * LANES)
            em_own[z : z + 1, lanes] = em[halo + x : halo + x + 1, :]
            cot_own[z : z + 1, lanes] = cot[outer + x : outer + x + 1, :]


def image_and_halo(plan, grid, copies, position, parts):
    f32 = jnp.float32
    rows = plan.x(plan.halo_in) + plan.x(plan.halo_last)
    own = jax.ShapeDtypeStruct((plan.zs, plan.xs * LANES), f32)
    vmem = pl.BlockSpec(memory_space=pltpu.VMEM)
    return pl.pallas_call(
        lambda *refs: image_kernel(plan, grid, copies, *refs),
        out_shape=[jax.ShapeDtypeStruct((copies, plan.zs, rows, LANES), jnp.bfloat16), own, own],
        in_specs=[pl.BlockSpec(memory_space=pltpu.SMEM), vmem],
        out_specs=[vmem] * 3,
        compiler_params=pltpu.CompilerParams(vmem_limit_bytes=VMEM_BYTES),
        name="image_and_halo",
    )(position, parts)


def grad_rows(plan):
    return ((plan.layers - 1) * (round_up(27 * plan.c, LANES) // LANES) + 2) * plan.c


def unpack_kernel(plan, factor, halves, grad_in, grad_mid, grad_out):
    c, mids = plan.c, plan.layers - 1
    block, per, rows = round_up(27 * c, LANES) // LANES, LANES // c, halves.shape[2]

    def packed(first):
        pieces = []
        for at in range(first, first + c, 8):
            slab, inner = divmod(at, CORES * rows)
            core, row = divmod(inner, rows)
            pieces.append(halves[core, slab, row : row + 8, :])
        return jnp.concatenate(pieces, axis=0) * factor

    for layer in range(mids):
        for k in range(block):
            lanes = packed((layer * block + k) * c)
            for tap in range(min(per, 27 - k * per)):
                grad_mid[layer * 27 + k * per + tap] = lanes[:, tap * c : (tap + 1) * c]
    for index, out in enumerate((grad_in, grad_out)):
        taps = packed((mids * block + index) * c).T
        for dz in range(3):
            for k in range(9):
                tap = dz * 9 + k
                out[26 - tap if index else tap] = taps[k * 8 + dz : k * 8 + dz + 1, :]


def unpack_grads(plan, halves, factor):
    c, mids = plan.c, plan.layers - 1
    f32 = jnp.float32
    thin = jax.ShapeDtypeStruct((27, 1, c), f32)
    vmem = pl.BlockSpec(memory_space=pltpu.VMEM)
    grad_in, mid, grad_out = pl.pallas_call(
        lambda *refs: unpack_kernel(plan, factor, *refs),
        out_shape=[thin, jax.ShapeDtypeStruct((mids * 27, c, c), f32), thin],
        in_specs=[vmem],
        out_specs=[vmem] * 3,
        compiler_params=pltpu.CompilerParams(vmem_limit_bytes=VMEM_BYTES),
        name="unpack_gradients",
    )(halves)
    mid = jnp.transpose(mid.reshape(mids, 3, 3, 3, c, c), (0, 4, 5, 1, 2, 3))
    grad_in = jnp.transpose(grad_in.reshape(3, 3, 3, 1, c), (4, 3, 0, 1, 2))
    grad_out = jnp.transpose(grad_out.reshape(3, 3, 3, 1, c), (3, 4, 0, 1, 2))
    return grad_in, mid, grad_out


CORES = 2


def along_chips(axis):
    count = lax.axis_size(axis)
    return [list(range(core, count, CORES)) for core in range(CORES)]


def within_chip(axis):
    count = lax.axis_size(axis)
    return [list(range(first, first + CORES)) for first in range(0, count, CORES)]


def to_all(value, axis, groups=None):
    count = lax.axis_size(axis) if groups is None else len(groups[0])
    copies = jnp.broadcast_to(value[None], (count, *value.shape))
    return lax.all_to_all(copies, axis, 0, 0, tiled=True, axis_index_groups=groups)


def pair_gather(value):
    return lax.all_gather(value, "sector", axis_index_groups=within_chip("sector"))


def summed_everywhere(packed, slabs, beside):
    chips = along_chips("sector")
    core = lax.rem(lax.axis_index("sector"), CORES)
    share = packed.shape[0] // slabs
    parts = packed.reshape(slabs, share, LANES)
    own = jnp.sum(lax.all_to_all(parts, "slab", 0, 0, tiled=True), axis=0)
    both = pair_gather(own)
    own = both[0] + both[1]
    half = lax.dynamic_slice_in_dim(own, core * (share // CORES), share // CORES, 0)
    half = to_all(half.astype(jnp.bfloat16), "sector", chips)
    half, beside = lax.optimization_barrier((half, beside))
    half = jnp.sum(half.astype(jnp.float32), axis=0)
    return pair_gather(to_all(half, "slab")), beside


def shards(
    image,
    sensitivity,
    tile_values,
    tile_rows,
    tile_cols,
    tile_count,
    measured,
    background,
    w_in,
    w_mid,
    w_out,
    cotangent,
):
    f32, bf16 = jnp.float32, jnp.bfloat16
    highest = lax.Precision.HIGHEST
    sectors, slabs = lax.axis_size("sector"), lax.axis_size("slab")
    sector, slab = lax.axis_index("sector"), lax.axis_index("slab")
    zs, xs, ys = image.shape
    block_len = xs * ys
    line_blocks, row_len = measured.shape[1:]
    slots = tile_rows.shape[1]
    plan = Plan(zs, xs, w_in.shape[0], w_mid.shape[0] + 1)
    grid = (zs * slabs, xs * sectors)

    cells = zs * xs
    chips = along_chips("sector")
    cols_row = jnp.pad(tile_cols.astype(bf16), ((0, round_up(cells + 1, 8) - cells - 1), (0, ys - slots)))
    sent = jnp.concatenate([image.astype(bf16).reshape(cells, ys), cols_row], axis=0)
    from_chips = to_all(sent, "sector", chips)
    every_cols = from_chips[:, cells, :slots].astype(f32).reshape(-1)
    got = pair_gather(from_chips[:, :cells])
    got = jnp.transpose(got.reshape(CORES, len(chips[0]), zs, xs, ys), (2, 1, 0, 3, 4))
    blocks = got.reshape(zs * sectors, block_len)

    fields = jnp.concatenate([field.reshape(cells, ys) for field in (image, sensitivity, cotangent)], axis=0)
    fields = jnp.pad(fields, ((0, round_up(3 * cells, 8) - 3 * cells), (0, 0)))
    fields, from_chips = lax.optimization_barrier((fields, from_chips))
    reach = -(-plan.halo_in // (xs * CORES))
    near_fields = []
    for chip in range(-reach, reach + 1):
        step = chip * CORES
        pairs = [(k + step, k) for k in range(sectors) if 0 <= k + step < sectors]
        near_fields.append(lax.ppermute(fields, "sector", pairs) if chip else fields)
    near_fields = jnp.concatenate([field[: 3 * cells] for field in near_fields], axis=0)

    values = tile_values[0]
    weight = (jnp.arange(slots) < tile_count[0, 0]).astype(f32) / block_len
    forward = jnp.einsum("krv,kv->kr", values, blocks[tile_cols[0]], preferred_element_type=f32)
    forward = forward * weight[:, None]
    lined = jnp.concatenate([forward, tile_rows[0].astype(f32)[:, None]], axis=1)
    lined = jnp.pad(lined, ((0, 0), (0, LANES - row_len - 1)))
    lined, *kernels = lax.optimization_barrier((lined, w_in, w_mid, w_out))
    weights = prepared_weights(plan, *kernels)
    every = to_all(lined, "slab").reshape(slabs * slots, LANES)
    every_rows = every[:, row_len]
    placing = (every_rows[None, :] == jnp.arange(line_blocks, dtype=f32)[:, None]).astype(f32)
    projection = jnp.dot(placing, every[:, :row_len], precision=highest)
    ratio = (measured[0] / (projection + background[0])).astype(bf16)

    backward = jnp.einsum("krv,kr->kv", values, ratio[tile_rows[0]], preferred_element_type=f32)
    backward = backward * weight[:, None]
    backward, weights = lax.optimization_barrier((backward, weights))
    every_back = to_all(backward, "sector", chips).reshape(-1, block_len)
    core = lax.rem(sector, CORES)
    span = (2 * reach + 1) * CORES
    near = sector - core - reach * CORES + jnp.arange(span)
    wanted = (jnp.arange(zs)[:, None] * sectors + near[None, :]).astype(f32)
    good = jnp.logical_and(near >= 0, near < sectors)
    wanted = jnp.where(good[None, :], wanted, -1.0).reshape(-1)
    owning = (every_cols[None, :] == wanted[:, None]).astype(f32)
    of_core = jnp.dot(owning, every_back, precision=highest).reshape(-1, ys)
    of_cores = pair_gather(jnp.concatenate([of_core, near_fields], axis=0))
    position = jnp.stack([slab * zs, sector * xs]).astype(jnp.int32)
    to_send, em_own, cot_own = image_and_halo(plan, grid, slabs, position, of_cores)

    received = lax.all_to_all(to_send, "slab", 0, 0, tiled=True)
    received = received.reshape(zs * slabs, *received.shape[2:])
    new_image, em_grad, packed = network(
        plan,
        grid,
        position,
        received,
        em_own,
        cot_own,
        weights,
        round_up(grad_rows(plan), slabs * CORES * 8),
    )
    new_image = new_image.reshape(zs, xs, ys)
    em_grad = em_grad.reshape(zs, xs, ys)
    halves, new_image = summed_everywhere(packed, slabs, new_image)
    factor = 1.0 / math.sqrt(grid[0] * grid[1] * ys)
    grad_in, grad_mid, grad_out = unpack_grads(plan, halves, factor)
    return (
        new_image,
        em_grad,
        grad_in,
        grad_mid,
        grad_out,
    )


def solution(mesh):
    placed = (
        P("slab", "sector", None),
        P("slab", "sector", None),
        P("sector", "slab", None, None),
        P("sector", "slab"),
        P("sector", "slab"),
        P("sector", "slab"),
        P("sector", None, None),
        P("sector", None, None),
        P(),
        P(),
        P(),
        P("slab", "sector", None),
    )
    return jax.shard_map(
        shards,
        mesh=mesh,
        in_specs=placed,
        out_specs=(P("slab", "sector", None), P("slab", "sector", None), P(), P(), P()),
        check_vma=False,
    )
```

```python
import math

import jax
import jax.numpy as jnp
from jax import lax
from jax.experimental import pallas as pl
from jax.experimental.pallas import tpu as pltpu
from jax.sharding import PartitionSpec as P

LANES = 128
VMEM_BYTES = 36 * 1024 * 1024
SMALL_VMEM_BYTES = 12 * 1024 * 1024


class Plan:
    def __init__(self, zs, xs, channels, layers):
        self.zs, self.xs, self.c, self.layers = zs, xs, channels, layers
        self.halo_u = [2 * layers - l + 1 for l in range(1, layers + 2)]
        self.halo_c = [l for l in range(1, layers + 1)]
        self.halo_in = 2 * layers
        self.halo_last = layers + 1
        self.lead_in = -(self.halo_in - 1) % 8
        self.lead_last = -(self.halo_last - 1) % 8
        self.rows_in = -(-(zs + 2 * self.halo_in + self.lead_in) // 8) * 8
        self.rows_last = -(-(zs + 2 * self.halo_last + self.lead_last) // 8) * 8

    def z(self, halo):
        return self.zs + 2 * halo

    def x(self, halo):
        return self.xs + 2 * halo

    def starts(self, planes):
        count = -(-planes // 2)
        size = -(-planes // count)
        return size, [min(k * size, planes - size) for k in range(count)]


def round_up(value, step):
    return -(-value // step) * step


def shifts(rows):
    lane = lax.broadcasted_iota(jnp.int32, rows.shape, 1)
    low = jnp.where(lane == 0, jnp.zeros_like(rows), pltpu.roll(rows, 1, 1))
    high = jnp.where(lane == LANES - 1, jnp.zeros_like(rows), pltpu.roll(rows, LANES - 1, 1))
    return low, rows, high


def prepare_kernel(plan, w_in, w_mid, w_out, *outs):
    w_first, w_top, w_last, w_back = outs[:4]
    toeplitz = outs[4:]
    c, zs, mids = plan.c, plan.zs, plan.layers - 1
    f32, bf16 = jnp.float32, jnp.bfloat16

    def rolled(rows, out, step, planes, first=0):
        for k in range(planes):
            moved = rows if k == 0 else pltpu.roll(rows, k * step, 1)
            out[(first + k) * c : (first + k + 1) * c, :] = moved.astype(bf16)

    for weights, out, rows, lead, planes, mirrored in (
        (w_in, w_first, plan.rows_in, plan.lead_in, plan.z(plan.halo_u[1]), False),
        (w_out, w_top, plan.rows_last, plan.lead_last, plan.z(plan.halo_c[-1]), True),
    ):
        tap = lax.broadcasted_iota(jnp.int32, (27, out.shape[1]), 0)
        tap = 26 - tap if mirrored else tap
        at = lax.rem(tap, 9) * rows + lead + lax.div(tap, 9)
        lane = lax.broadcasted_iota(jnp.int32, at.shape, 1)
        chosen = jnp.where(lane == at, 1.0, 0.0).astype(bf16)
        base = lax.dot_general(
            weights[...], chosen, (((0,), (0,)), ((), ())), preferred_element_type=f32
        )
        rolled(base, out, 1, planes)

    def spread(tile, taps, planes, width):
        pieces = []
        for k in taps:
            pieces += [tile(0, k), tile(1, k), tile(2, k)]
            lines = pieces[0].shape[0]
            pieces.append(jnp.zeros((lines, (planes - 3) * c), f32))
        rest = width - len(taps) * planes * c
        if rest:
            pieces.append(jnp.zeros((lines, rest), f32))
        return jnp.concatenate(pieces, axis=1)

    for weights, out, mirrored in ((w_out, w_last, False), (w_in, w_back, True)):
        lines = weights[...].astype(f32)

        def row(dz, k, lines=lines, mirrored=mirrored):
            tap = 26 - dz * 9 - k if mirrored else dz * 9 + k
            return lines[tap : tap + 1, :]

        rows = jnp.broadcast_to(spread(row, range(9), zs + 2, out.shape[1]), out.shape)
        line = lax.broadcasted_iota(jnp.int32, rows.shape, 0)
        total = jnp.where(line == 0, rows, 0.0)
        for k in range(1, zs):
            total = total + jnp.where(line == k, pltpu.roll(rows, k * c, 1), 0.0)
        out[...] = total.astype(bf16)

    for index, out in enumerate(toeplitz):
        first = (index % mids) * 27

        def tile(dz, k, first=first, mirrored=index >= mids):
            if mirrored:
                return w_mid[first + 26 - dz * 9 - k].astype(f32).T
            return w_mid[first + dz * 9 + k].astype(f32)

        size = out.shape[0] // (3 * c)
        for dx in range(3):
            rows = spread(tile, range(dx * 3, dx * 3 + 3), size + 2, out.shape[1])
            rolled(rows, out, c, size, dx * size)


def inside(first, count, c, bound):
    line = lax.broadcasted_iota(jnp.int32, (count * c, 1), 0)
    plane = first + lax.shift_right_arithmetic(line, int(math.log2(c)))
    return jnp.logical_and(plane >= 0, plane < bound)


def network_kernel(plan, grid, pos, received, em_own, cot_own, w_first, w_top, w_out, w_back, *refs):
    layers, c, zs, xs = plan.layers, plan.c, plan.zs, plan.xs
    mids = layers - 1
    w_fwd, w_bwd = refs[:mids], refs[mids : 2 * mids]
    new_image, em_grad, grads = refs[2 * mids : 2 * mids + 3]
    scratch = refs[2 * mids + 3 :]
    first_sh, last_sh = scratch[:2]
    u_sh = scratch[2 : 2 + layers]
    pre = scratch[2 + layers : 2 + 2 * layers]
    c_sh = scratch[2 + 2 * layers : 2 + 3 * layers]
    z_first, x_first = pos[0], pos[1]
    f32, bf16 = jnp.float32, jnp.bfloat16

    wide = plan.x(plan.halo_in)
    for target, gathered, halo, lead, first_row in (
        (first_sh, scratch[-2], plan.halo_in, plan.lead_in, 0),
        (last_sh, scratch[-1], plan.halo_last, plan.lead_last, wide),
    ):
        gathered[...] = jnp.zeros(gathered.shape, f32)
        for k in range(plan.z(halo)):
            plane = z_first - halo + k
            inner = jnp.logical_and(plane >= 0, plane < grid[0])
            rows = received[jnp.clip(plane, 0, grid[0] - 1)].astype(f32)
            rows = jnp.where(inner, rows, 0.0)
            for x in range(plan.x(halo)):
                span = slice(x * LANES, (x + 1) * LANES)
                gathered[lead + k : lead + k + 1, span] = rows[first_row + x : first_row + x + 1, :]
        for x in range(plan.x(halo)):
            span = slice(x * LANES, (x + 1) * LANES)
            for dy, rows in enumerate(shifts(gathered[:, span])):
                target[dy, :, span] = rows

    def store_shifted(target, value, rows, lane, x_at, keep):
        for half in range(2):
            part = value[:, half * LANES : (half + 1) * LANES]
            good = jnp.logical_and(x_at + half >= 0, x_at + half < grid[1])
            part = jnp.where(jnp.logical_and(keep, good), part, 0.0).astype(bf16)
            for dy, moved in enumerate(shifts(part)):
                target[dy, rows, lane + half * LANES : lane + (half + 1) * LANES] = moved

    def one_channel(source, weight, lane):
        pieces = [
            source[dy, :, lane + dx * LANES : lane + (dx + 2) * LANES] for dx in range(3) for dy in range(3)
        ]
        stacked = jnp.concatenate(pieces, axis=0).astype(bf16)
        return jnp.dot(weight[:, : stacked.shape[0]], stacked, preferred_element_type=f32)

    def many_channels(source, weight, first_plane, planes, count):
        rows = slice(first_plane * c, (first_plane + planes + 2) * c)
        lines = planes * c

        def product(pair):
            span = slice(pair * 2 * LANES, (pair + 1) * 2 * LANES)
            stacked = jnp.concatenate([source[dy, rows, span] for dy in range(3)], axis=0)
            return jnp.dot(weight[:, : stacked.shape[0]], stacked, preferred_element_type=f32)

        left = product(0)
        for pair in range(count):
            right = product(pair + 1)
            middle = [left[lines : 2 * lines, LANES:], right[lines : 2 * lines, :LANES]]
            yield left[:lines] + jnp.concatenate(middle, axis=1) + right[2 * lines :]
            left = right

    def forward_tail(value, layer, first_plane, planes, pair, lane):
        halo = plan.halo_u[layer]
        rows = slice(first_plane * c, (first_plane + planes) * c)
        near = plan.halo_c[layer - 1]
        edge = halo - near
        low, high = max(first_plane, edge), min(first_plane + planes, edge + plan.z(near))
        at = lane - edge * LANES
        if low < high and 0 <= at < plan.x(near) * LANES:
            kept = value[(low - first_plane) * c : (high - first_plane) * c]
            pre[layer - 1][(low - edge) * c : (high - edge) * c, at : at + 2 * LANES] = kept
        act = value * jax.nn.sigmoid(value)
        keep = inside(z_first - halo + first_plane, planes, c, grid[0])
        store_shifted(u_sh[layer - 1], act, rows, lane, x_first - halo + 2 * pair, keep)

    def backward_tail(value, layer, first_plane, planes, pair, lane):
        halo = plan.halo_c[layer - 1]
        rows = slice(first_plane * c, (first_plane + planes) * c)
        preact = pre[layer - 1][rows, lane : lane + 2 * LANES]
        sigma = jax.nn.sigmoid(preact)
        slope = sigma * (1.0 + preact * (1.0 - sigma))
        keep = inside(z_first - halo + first_plane, planes, c, grid[0])
        store_shifted(
            c_sh[layer - 1], slope * value, rows, lane, x_first - halo + 2 * pair, keep
        )

    halo = plan.halo_u[1]
    for pair in range(plan.x(halo) // 2):
        lane = pair * 2 * LANES
        forward_tail(one_channel(first_sh, w_first, lane), 1, 0, plan.z(halo), pair, lane)
    for layer in range(2, layers + 1):
        halo = plan.halo_u[layer]
        size, starts = plan.starts(plan.z(halo))
        for start in starts:
            values = many_channels(
                u_sh[layer - 2], w_fwd[layer - 2], start, size, plan.x(halo) // 2
            )
            for pair, value in enumerate(values):
                forward_tail(value, layer, start, size, pair, pair * 2 * LANES)

    def own_taps(source, halo):
        rows = slice((halo - 1) * c, (halo + zs + 1) * c)
        pieces = [
            source[dy, rows, (halo - 1 + dx) * LANES : (halo - 1 + dx + xs) * LANES]
            for dx in range(3)
            for dy in range(3)
        ]
        return jnp.concatenate(pieces, axis=0)

    top = plan.halo_u[layers]
    taps = own_taps(u_sh[layers - 1], top)
    last = jnp.dot(w_out[:, : taps.shape[0]], taps, preferred_element_type=f32)
    new_image[...] = em_own[...] + last[:zs, :]

    halo = plan.halo_c[-1]

    for pair in range(plan.x(halo) // 2):
        lane = pair * 2 * LANES
        backward_tail(one_channel(last_sh, w_top, lane), layers, 0, plan.z(halo), pair, lane)
    for layer in range(layers - 1, 0, -1):
        halo = plan.halo_c[layer - 1]
        size, starts = plan.starts(plan.z(halo))
        for start in starts:
            values = many_channels(c_sh[layer], w_bwd[layer - 1], start, size, plan.x(halo) // 2)
            for pair, value in enumerate(values):
                backward_tail(value, layer, start, size, pair, pair * 2 * LANES)
    taps = own_taps(c_sh[0], plan.halo_c[0])
    down = jnp.dot(w_back[:, : taps.shape[0]], taps, preferred_element_type=f32)
    em_grad[...] = cot_own[...] + down[:zs, :]

    def own_rows(source, halo, plane):
        return source[1, (halo + plane) * c : (halo + plane + 1) * c, halo * LANES : (halo + xs) * LANES]

    def against(cells, taps):
        return lax.dot_general(cells, taps, (((1,), (1,)), ((), ())), preferred_element_type=f32)

    block = round_up(27 * c, LANES) // LANES
    for layer in range(2, layers + 1):
        source, halo = u_sh[layer - 2], plan.halo_u[layer - 1]
        total = None
        for plane in range(zs):
            first = halo - 1 + plane
            pieces = [
                source[
                    dy,
                    (first + dz) * c : (first + dz + 1) * c,
                    (halo - 1 + dx) * LANES : (halo - 1 + dx + xs) * LANES,
                ]
                for dz in range(3)
                for dx in range(3)
                for dy in range(3)
            ]
            pieces.append(jnp.zeros((block * LANES - 27 * c, xs * LANES), bf16))
            cells = own_rows(c_sh[layer - 1], plan.halo_c[layer - 1], plane)
            term = against(cells, jnp.concatenate(pieces, axis=0))
            total = term if total is None else total + term
        for k in range(block):
            at = ((layer - 2) * block + k) * c
            grads[at : at + c, :] = total[:, k * LANES : (k + 1) * LANES]

    def thin(source, halo, lead, cells_of, at):
        row = lead + halo - 1
        pieces = [
            source[dy, row : row + 8, (halo - 1 + dx) * LANES : (halo - 1 + dx + xs) * LANES]
            for dx in range(3)
            for dy in range(3)
        ]
        pieces.append(jnp.zeros((LANES - 72, xs * LANES), f32))
        taps = jnp.concatenate(pieces, axis=0).astype(bf16)
        total = None
        for plane in range(zs):
            term = against(cells_of(plane), taps)
            if plane:
                term = pltpu.roll(term, LANES - plane, 1)
            total = term if total is None else total + term
        grads[at : at + c, :] = total

    thin(
        first_sh,
        plan.halo_in,
        plan.lead_in,
        lambda plane: own_rows(c_sh[0], plan.halo_c[0], plane),
        mids * block * c,
    )
    thin(
        last_sh,
        plan.halo_last,
        plan.lead_last,
        lambda plane: own_rows(u_sh[layers - 1], top, plane),
        (mids * block + 1) * c,
    )
    used = (mids * block + 2) * c
    if used < grads.shape[0]:
        grads[used:, :] = jnp.zeros((grads.shape[0] - used, LANES), f32)


def prepared_weights(plan, w_in, w_mid, w_out):
    c, mids = plan.c, plan.layers - 1
    bf16 = jnp.bfloat16

    def banded(halo):
        size, _ = plan.starts(plan.z(halo))
        return (3 * size * c, round_up(3 * (size + 2) * c, LANES))

    last = (8, round_up(9 * (plan.zs + 2) * c, LANES))
    shapes = [
        (plan.z(plan.halo_u[1]) * c, round_up(9 * plan.rows_in, LANES)),
        (plan.z(plan.halo_c[-1]) * c, round_up(9 * plan.rows_last, LANES)),
        last,
        last,
    ]
    shapes += [banded(plan.halo_u[k + 2]) for k in range(mids)]
    shapes += [banded(plan.halo_c[k]) for k in range(mids)]
    vmem = pl.BlockSpec(memory_space=pltpu.VMEM)
    return pl.pallas_call(
        lambda *refs: prepare_kernel(plan, *refs),
        out_shape=[jax.ShapeDtypeStruct(shape, bf16) for shape in shapes],
        in_specs=[vmem] * 3,
        out_specs=[vmem] * len(shapes),
        compiler_params=pltpu.CompilerParams(vmem_limit_bytes=SMALL_VMEM_BYTES),
        name="prepare_weights",
    )(
        jnp.transpose(w_in, (2, 3, 4, 1, 0)).reshape(27, c),
        jnp.transpose(w_mid, (0, 3, 4, 5, 1, 2)).reshape(mids * 27, c, c),
        jnp.transpose(w_out, (2, 3, 4, 0, 1)).reshape(27, c),
    )


def network(plan, grid, position, received, em_own, cot_own, weights, packed_rows):
    layers, c = plan.layers, plan.c
    f32, bf16 = jnp.float32, jnp.bfloat16
    own = jax.ShapeDtypeStruct((plan.zs, plan.xs * LANES), f32)
    scratch = [
        pltpu.VMEM((3, plan.rows_in, plan.x(plan.halo_in) * LANES), f32),
        pltpu.VMEM((3, plan.rows_last, plan.x(plan.halo_last) * LANES), f32),
    ]

    def region(halo, lead=()):
        return (*lead, plan.z(halo) * c, plan.x(halo) * LANES)

    scratch += [pltpu.VMEM(region(plan.halo_u[l], (3,)), bf16) for l in range(1, layers + 1)]
    scratch += [pltpu.VMEM(region(plan.halo_c[l - 1]), f32) for l in range(1, layers + 1)]
    scratch += [pltpu.VMEM(region(plan.halo_c[l - 1], (3,)), bf16) for l in range(1, layers + 1)]
    vmem = pl.BlockSpec(memory_space=pltpu.VMEM)
    scratch += [
        pltpu.VMEM((plan.rows_in, plan.x(plan.halo_in) * LANES), f32),
        pltpu.VMEM((plan.rows_last, plan.x(plan.halo_last) * LANES), f32),
    ]
    operands = (position, received, em_own, cot_own, *weights)
    return pl.pallas_call(
        lambda *refs: network_kernel(plan, grid, *refs),
        out_shape=[own, own, jax.ShapeDtypeStruct((packed_rows, LANES), f32)],
        in_specs=[pl.BlockSpec(memory_space=pltpu.SMEM)] + [vmem] * (len(operands) - 1),
        out_specs=[vmem] * 3,
        scratch_shapes=scratch,
        compiler_params=pltpu.CompilerParams(vmem_limit_bytes=VMEM_BYTES),
        name="network",
    )(*operands)


def image_kernel(plan, grid, copies, pos, parts, sent, em_own, cot_own):
    zs, xs, halo, outer = plan.zs, plan.xs, plan.halo_in, plan.halo_last
    reach = -(-halo // (xs * CORES))
    span = (2 * reach + 1) * CORES * xs
    x_first = pos[1]
    core = lax.rem(lax.div(x_first, xs), CORES)
    row = x_first - (core + reach * CORES) * xs + lax.broadcasted_iota(jnp.int32, (span, LANES), 0)
    good = jnp.logical_and(row >= 0, row < grid[1])

    def near(field, z):
        pieces = []
        for chip in range(2 * reach + 1):
            at = zs * span + (chip * 3 + field) * zs * xs + z * xs
            pieces += [parts[k, at : at + xs, :] for k in range(CORES)]
        return jnp.concatenate(pieces, axis=0)

    def window(rows, halo):
        first = reach * CORES * xs - halo
        count = xs + 2 * halo
        taken = rows[first : first + count]
        for k in range(1, CORES):
            taken = jnp.where(core == k, rows[first + k * xs : first + k * xs + count], taken)
        return taken

    for z in range(zs):
        back = parts[0, z * span : (z + 1) * span, :]
        for k in range(1, CORES):
            back = back + parts[k, z * span : (z + 1) * span, :]
        em = window(jnp.where(good, near(0, z) * back / near(1, z), 0.0), halo)
        cot = window(jnp.where(good, near(2, z), 0.0), outer)
        both = jnp.concatenate([em, cot], axis=0).astype(jnp.bfloat16)
        for k in range(copies):
            sent[k, z] = both
        for x in range(xs):
            lanes = slice(x * LANES, (x + 1) * LANES)
            em_own[z : z + 1, lanes] = em[halo + x : halo + x + 1, :]
            cot_own[z : z + 1, lanes] = cot[outer + x : outer + x + 1, :]


def image_and_halo(plan, grid, copies, position, parts):
    f32 = jnp.float32
    rows = plan.x(plan.halo_in) + plan.x(plan.halo_last)
    own = jax.ShapeDtypeStruct((plan.zs, plan.xs * LANES), f32)
    vmem = pl.BlockSpec(memory_space=pltpu.VMEM)
    return pl.pallas_call(
        lambda *refs: image_kernel(plan, grid, copies, *refs),
        out_shape=[jax.ShapeDtypeStruct((copies, plan.zs, rows, LANES), jnp.bfloat16), own, own],
        in_specs=[pl.BlockSpec(memory_space=pltpu.SMEM), vmem],
        out_specs=[vmem] * 3,
        compiler_params=pltpu.CompilerParams(vmem_limit_bytes=SMALL_VMEM_BYTES),
        name="image_and_halo",
    )(position, parts)


def grad_rows(plan):
    return ((plan.layers - 1) * (round_up(27 * plan.c, LANES) // LANES) + 2) * plan.c


def unpack_kernel(plan, factor, halves, grad_in, grad_mid, grad_out):
    c, mids = plan.c, plan.layers - 1
    block, per, rows = round_up(27 * c, LANES) // LANES, LANES // c, halves.shape[2]

    def packed(first):
        pieces = []
        for at in range(first, first + c, 8):
            slab, inner = divmod(at, CORES * rows)
            core, row = divmod(inner, rows)
            pieces.append(halves[core, slab, row : row + 8, :])
        return jnp.concatenate(pieces, axis=0) * factor

    for layer in range(mids):
        for k in range(block):
            lanes = packed((layer * block + k) * c)
            for tap in range(min(per, 27 - k * per)):
                grad_mid[layer * 27 + k * per + tap] = lanes[:, tap * c : (tap + 1) * c]
    for index, out in enumerate((grad_in, grad_out)):
        taps = packed((mids * block + index) * c).T
        for dz in range(3):
            for k in range(9):
                tap = dz * 9 + k
                out[26 - tap if index else tap] = taps[k * 8 + dz : k * 8 + dz + 1, :]


def unpack_grads(plan, halves, factor):
    c, mids = plan.c, plan.layers - 1
    f32 = jnp.float32
    thin = jax.ShapeDtypeStruct((27, 1, c), f32)
    vmem = pl.BlockSpec(memory_space=pltpu.VMEM)
    grad_in, mid, grad_out = pl.pallas_call(
        lambda *refs: unpack_kernel(plan, factor, *refs),
        out_shape=[thin, jax.ShapeDtypeStruct((mids * 27, c, c), f32), thin],
        in_specs=[vmem],
        out_specs=[vmem] * 3,
        compiler_params=pltpu.CompilerParams(vmem_limit_bytes=SMALL_VMEM_BYTES),
        name="unpack_gradients",
    )(halves)
    mid = jnp.transpose(mid.reshape(mids, 3, 3, 3, c, c), (0, 4, 5, 1, 2, 3))
    grad_in = jnp.transpose(grad_in.reshape(3, 3, 3, 1, c), (4, 3, 0, 1, 2))
    grad_out = jnp.transpose(grad_out.reshape(3, 3, 3, 1, c), (3, 4, 0, 1, 2))
    return grad_in, mid, grad_out


CORES = 2


def along_chips(axis):
    count = lax.axis_size(axis)
    return [list(range(core, count, CORES)) for core in range(CORES)]


def within_chip(axis):
    count = lax.axis_size(axis)
    return [list(range(first, first + CORES)) for first in range(0, count, CORES)]


def to_all(value, axis, groups=None):
    count = lax.axis_size(axis) if groups is None else len(groups[0])
    copies = jnp.broadcast_to(value[None], (count, *value.shape))
    return lax.all_to_all(copies, axis, 0, 0, tiled=True, axis_index_groups=groups)


def pair_gather(value):
    return lax.all_gather(value, "sector", axis_index_groups=within_chip("sector"))


def summed_everywhere(packed, slabs, beside):
    chips = along_chips("sector")
    core = lax.rem(lax.axis_index("sector"), CORES)
    share = packed.shape[0] // slabs
    parts = packed.reshape(slabs, share, LANES)
    own = jnp.sum(lax.all_to_all(parts, "slab", 0, 0, tiled=True), axis=0)
    both = pair_gather(own)
    own = both[0] + both[1]
    half = lax.dynamic_slice_in_dim(own, core * (share // CORES), share // CORES, 0)
    half = to_all(half.astype(jnp.bfloat16), "sector", chips)
    half, beside = lax.optimization_barrier((half, beside))
    half = jnp.sum(half.astype(jnp.float32), axis=0)
    return pair_gather(to_all(half, "slab")), beside


def shards(
    image,
    sensitivity,
    tile_values,
    tile_rows,
    tile_cols,
    tile_count,
    measured,
    background,
    w_in,
    w_mid,
    w_out,
    cotangent,
):
    f32, bf16 = jnp.float32, jnp.bfloat16
    highest = lax.Precision.HIGHEST
    sectors, slabs = lax.axis_size("sector"), lax.axis_size("slab")
    sector, slab = lax.axis_index("sector"), lax.axis_index("slab")
    zs, xs, ys = image.shape
    block_len = xs * ys
    line_blocks, row_len = measured.shape[1:]
    slots = tile_rows.shape[1]
    plan = Plan(zs, xs, w_in.shape[0], w_mid.shape[0] + 1)
    grid = (zs * slabs, xs * sectors)

    cells = zs * xs
    chips = along_chips("sector")
    cols_row = jnp.pad(tile_cols.astype(bf16), ((0, round_up(cells + 1, 8) - cells - 1), (0, ys - slots)))
    sent = jnp.concatenate([image.astype(bf16).reshape(cells, ys), cols_row], axis=0)
    from_chips = to_all(sent, "sector", chips)
    every_cols = from_chips[:, cells, :slots].astype(f32).reshape(-1)
    got = pair_gather(from_chips[:, :cells])
    got = jnp.transpose(got.reshape(CORES, len(chips[0]), zs, xs, ys), (2, 1, 0, 3, 4))
    blocks = got.reshape(zs * sectors, block_len)

    fields = jnp.concatenate([field.reshape(cells, ys) for field in (image, sensitivity, cotangent)], axis=0)
    fields = jnp.pad(fields, ((0, round_up(3 * cells, 8) - 3 * cells), (0, 0)))
    fields, from_chips = lax.optimization_barrier((fields, from_chips))
    reach = -(-plan.halo_in // (xs * CORES))
    near_fields = []
    for chip in range(-reach, reach + 1):
        step = chip * CORES
        pairs = [(k + step, k) for k in range(sectors) if 0 <= k + step < sectors]
        near_fields.append(lax.ppermute(fields, "sector", pairs) if chip else fields)
    near_fields = jnp.concatenate([field[: 3 * cells] for field in near_fields], axis=0)

    values = tile_values[0]
    weight = (jnp.arange(slots) < tile_count[0, 0]).astype(f32) / block_len
    forward = jnp.einsum("krv,kv->kr", values, blocks[tile_cols[0]], preferred_element_type=f32)
    forward = forward * weight[:, None]
    lined = jnp.concatenate([forward, tile_rows[0].astype(f32)[:, None]], axis=1)
    lined = jnp.pad(lined, ((0, 0), (0, LANES - row_len - 1)))
    lined, *kernels = lax.optimization_barrier((lined, w_in, w_mid, w_out))
    weights = prepared_weights(plan, *kernels)
    every = to_all(lined, "slab").reshape(slabs * slots, LANES)
    every_rows = every[:, row_len]
    placing = (every_rows[None, :] == jnp.arange(line_blocks, dtype=f32)[:, None]).astype(f32)
    projection = jnp.dot(placing, every[:, :row_len], precision=highest)
    ratio = (measured[0] / (projection + background[0])).astype(bf16)

    backward = jnp.einsum("krv,kr->kv", values, ratio[tile_rows[0]], preferred_element_type=f32)
    backward = backward * weight[:, None]
    backward, weights = lax.optimization_barrier((backward, weights))
    every_back = to_all(backward, "sector", chips).reshape(-1, block_len)
    core = lax.rem(sector, CORES)
    span = (2 * reach + 1) * CORES
    near = sector - core - reach * CORES + jnp.arange(span)
    wanted = (jnp.arange(zs)[:, None] * sectors + near[None, :]).astype(f32)
    good = jnp.logical_and(near >= 0, near < sectors)
    wanted = jnp.where(good[None, :], wanted, -1.0).reshape(-1)
    owning = (every_cols[None, :] == wanted[:, None]).astype(f32)
    of_core = jnp.dot(owning, every_back, precision=highest).reshape(-1, ys)
    of_cores = pair_gather(jnp.concatenate([of_core, near_fields], axis=0))
    position = jnp.stack([slab * zs, sector * xs]).astype(jnp.int32)
    to_send, em_own, cot_own = image_and_halo(plan, grid, slabs, position, of_cores)

    received = lax.all_to_all(to_send, "slab", 0, 0, tiled=True)
    received = received.reshape(zs * slabs, *received.shape[2:])
    new_image, em_grad, packed = network(
        plan,
        grid,
        position,
        received,
        em_own,
        cot_own,
        weights,
        round_up(grad_rows(plan), slabs * CORES * 8),
    )
    new_image = new_image.reshape(zs, xs, ys)
    em_grad = em_grad.reshape(zs, xs, ys)
    halves, new_image = summed_everywhere(packed, slabs, new_image)
    factor = 1.0 / math.sqrt(grid[0] * grid[1] * ys)
    grad_in, grad_mid, grad_out = unpack_grads(plan, halves, factor)
    return (
        new_image,
        em_grad,
        grad_in,
        grad_mid,
        grad_out,
    )


def solution(mesh):
    placed = (
        P("slab", "sector", None),
        P("slab", "sector", None),
        P("sector", "slab", None, None),
        P("sector", "slab"),
        P("sector", "slab"),
        P("sector", "slab"),
        P("sector", None, None),
        P("sector", None, None),
        P(),
        P(),
        P(),
        P("slab", "sector", None),
    )
    return jax.shard_map(
        shards,
        mesh=mesh,
        in_specs=placed,
        out_specs=(P("slab", "sector", None), P("slab", "sector", None), P(), P(), P()),
        check_vma=False,
    )
```

```python
import math

import jax
import jax.numpy as jnp
from jax import lax
from jax.experimental import pallas as pl
from jax.experimental.pallas import tpu as pltpu
from jax.sharding import PartitionSpec as P

LANES = 128
VMEM_BYTES = 36 * 1024 * 1024
SMALL_VMEM_BYTES = 12 * 1024 * 1024


class Plan:
    def __init__(self, zs, xs, channels, layers):
        self.zs, self.xs, self.c, self.layers = zs, xs, channels, layers
        self.halo_u = [2 * layers - l + 1 for l in range(1, layers + 2)]
        self.halo_c = [l for l in range(1, layers + 1)]
        self.halo_in = 2 * layers
        self.halo_last = layers + 1
        self.lead_in = -(self.halo_in - 1) % 8
        self.lead_last = -(self.halo_last - 1) % 8
        self.rows_in = -(-(zs + 2 * self.halo_in + self.lead_in) // 8) * 8
        self.rows_last = -(-(zs + 2 * self.halo_last + self.lead_last) // 8) * 8

    def z(self, halo):
        return self.zs + 2 * halo

    def x(self, halo):
        return self.xs + 2 * halo

    def starts(self, planes):
        count = -(-planes // 2)
        size = -(-planes // count)
        return size, [min(k * size, planes - size) for k in range(count)]


def round_up(value, step):
    return -(-value // step) * step


def shifts(rows):
    lane = lax.broadcasted_iota(jnp.int32, rows.shape, 1)
    low = jnp.where(lane == 0, jnp.zeros_like(rows), pltpu.roll(rows, 1, 1))
    high = jnp.where(lane == LANES - 1, jnp.zeros_like(rows), pltpu.roll(rows, LANES - 1, 1))
    return low, rows, high


def prepare_kernel(plan, w_in, w_mid, w_out, *outs):
    w_first, w_top, w_last, w_back = outs[:4]
    toeplitz = outs[4:]
    c, zs, mids = plan.c, plan.zs, plan.layers - 1
    f32, bf16 = jnp.float32, jnp.bfloat16

    def rolled(rows, out, step, planes, first=0):
        for k in range(planes):
            moved = rows if k == 0 else pltpu.roll(rows, k * step, 1)
            out[(first + k) * c : (first + k + 1) * c, :] = moved.astype(bf16)

    for weights, out, rows, lead, planes, mirrored in (
        (w_in, w_first, plan.rows_in, plan.lead_in, plan.z(plan.halo_u[1]), False),
        (w_out, w_top, plan.rows_last, plan.lead_last, plan.z(plan.halo_c[-1]), True),
    ):
        tap = lax.broadcasted_iota(jnp.int32, (27, out.shape[1]), 0)
        tap = 26 - tap if mirrored else tap
        at = lax.rem(tap, 9) * rows + lead + lax.div(tap, 9)
        lane = lax.broadcasted_iota(jnp.int32, at.shape, 1)
        chosen = jnp.where(lane == at, 1.0, 0.0).astype(bf16)
        base = lax.dot_general(
            weights[...], chosen, (((0,), (0,)), ((), ())), preferred_element_type=f32
        )
        rolled(base, out, 1, planes)

    def spread(tile, taps, planes, width):
        pieces = []
        for k in taps:
            pieces += [tile(0, k), tile(1, k), tile(2, k)]
            lines = pieces[0].shape[0]
            pieces.append(jnp.zeros((lines, (planes - 3) * c), f32))
        rest = width - len(taps) * planes * c
        if rest:
            pieces.append(jnp.zeros((lines, rest), f32))
        return jnp.concatenate(pieces, axis=1)

    for weights, out, mirrored in ((w_out, w_last, False), (w_in, w_back, True)):
        lines = weights[...].astype(f32)

        def row(dz, k, lines=lines, mirrored=mirrored):
            tap = 26 - dz * 9 - k if mirrored else dz * 9 + k
            return lines[tap : tap + 1, :]

        rows = jnp.broadcast_to(spread(row, range(9), zs + 2, out.shape[1]), out.shape)
        line = lax.broadcasted_iota(jnp.int32, rows.shape, 0)
        total = jnp.where(line == 0, rows, 0.0)
        for k in range(1, zs):
            total = total + jnp.where(line == k, pltpu.roll(rows, k * c, 1), 0.0)
        out[...] = total.astype(bf16)

    for index, out in enumerate(toeplitz):
        first = (index % mids) * 27

        def tile(dz, k, first=first, mirrored=index >= mids):
            if mirrored:
                return w_mid[first + 26 - dz * 9 - k].astype(f32).T
            return w_mid[first + dz * 9 + k].astype(f32)

        size = out.shape[0] // (3 * c)
        for dx in range(3):
            rows = spread(tile, range(dx * 3, dx * 3 + 3), size + 2, out.shape[1])
            rolled(rows, out, c, size, dx * size)


def inside(first, count, c, bound):
    line = lax.broadcasted_iota(jnp.int32, (count * c, 1), 0)
    plane = first + lax.shift_right_arithmetic(line, int(math.log2(c)))
    return jnp.logical_and(plane >= 0, plane < bound)


def network_kernel(plan, grid, pos, received, em_own, cot_own, w_first, w_top, w_out, w_back, *refs):
    layers, c, zs, xs = plan.layers, plan.c, plan.zs, plan.xs
    mids = layers - 1
    w_fwd, w_bwd = refs[:mids], refs[mids : 2 * mids]
    new_image, em_grad, grads = refs[2 * mids : 2 * mids + 3]
    scratch = refs[2 * mids + 3 :]
    first_sh, last_sh = scratch[:2]
    u_sh = scratch[2 : 2 + layers]
    pre = scratch[2 + layers : 2 + 2 * layers]
    c_sh = scratch[2 + 2 * layers : 2 + 3 * layers]
    z_first, x_first = pos[0], pos[1]
    f32, bf16 = jnp.float32, jnp.bfloat16

    wide = plan.x(plan.halo_in)
    for target, gathered, halo, lead, first_row in (
        (first_sh, scratch[-2], plan.halo_in, plan.lead_in, 0),
        (last_sh, scratch[-1], plan.halo_last, plan.lead_last, wide),
    ):
        gathered[...] = jnp.zeros(gathered.shape, f32)
        for k in range(plan.z(halo)):
            plane = z_first - halo + k
            inner = jnp.logical_and(plane >= 0, plane < grid[0])
            rows = received[jnp.clip(plane, 0, grid[0] - 1)].astype(f32)
            rows = jnp.where(inner, rows, 0.0)
            for x in range(plan.x(halo)):
                span = slice(x * LANES, (x + 1) * LANES)
                gathered[lead + k : lead + k + 1, span] = rows[first_row + x : first_row + x + 1, :]
        for x in range(plan.x(halo)):
            span = slice(x * LANES, (x + 1) * LANES)
            for dy, rows in enumerate(shifts(gathered[:, span])):
                target[dy, :, span] = rows

    def store_shifted(target, value, rows, lane, x_at, keep):
        for half in range(2):
            part = value[:, half * LANES : (half + 1) * LANES]
            good = jnp.logical_and(x_at + half >= 0, x_at + half < grid[1])
            part = jnp.where(jnp.logical_and(keep, good), part, 0.0).astype(bf16)
            for dy, moved in enumerate(shifts(part)):
                target[dy, rows, lane + half * LANES : lane + (half + 1) * LANES] = moved

    def one_channel(source, weight, lane):
        pieces = [
            source[dy, :, lane + dx * LANES : lane + (dx + 2) * LANES] for dx in range(3) for dy in range(3)
        ]
        stacked = jnp.concatenate(pieces, axis=0).astype(bf16)
        return jnp.dot(weight[:, : stacked.shape[0]], stacked, preferred_element_type=f32)

    def many_channels(source, weight, first_plane, planes, count):
        rows = slice(first_plane * c, (first_plane + planes + 2) * c)
        lines = planes * c

        def product(pair):
            span = slice(pair * 2 * LANES, (pair + 1) * 2 * LANES)
            stacked = jnp.concatenate([source[dy, rows, span] for dy in range(3)], axis=0)
            return jnp.dot(weight[:, : stacked.shape[0]], stacked, preferred_element_type=f32)

        left = product(0)
        for pair in range(count):
            right = product(pair + 1)
            middle = [left[lines : 2 * lines, LANES:], right[lines : 2 * lines, :LANES]]
            yield left[:lines] + jnp.concatenate(middle, axis=1) + right[2 * lines :]
            left = right

    def forward_tail(value, layer, first_plane, planes, pair, lane):
        halo = plan.halo_u[layer]
        rows = slice(first_plane * c, (first_plane + planes) * c)
        near = plan.halo_c[layer - 1]
        edge = halo - near
        low, high = max(first_plane, edge), min(first_plane + planes, edge + plan.z(near))
        at = lane - edge * LANES
        if low < high and 0 <= at < plan.x(near) * LANES:
            kept = value[(low - first_plane) * c : (high - first_plane) * c]
            pre[layer - 1][(low - edge) * c : (high - edge) * c, at : at + 2 * LANES] = kept
        act = value * jax.nn.sigmoid(value)
        keep = inside(z_first - halo + first_plane, planes, c, grid[0])
        store_shifted(u_sh[layer - 1], act, rows, lane, x_first - halo + 2 * pair, keep)

    def backward_tail(value, layer, first_plane, planes, pair, lane):
        halo = plan.halo_c[layer - 1]
        rows = slice(first_plane * c, (first_plane + planes) * c)
        preact = pre[layer - 1][rows, lane : lane + 2 * LANES]
        sigma = jax.nn.sigmoid(preact)
        slope = sigma * (1.0 + preact * (1.0 - sigma))
        keep = inside(z_first - halo + first_plane, planes, c, grid[0])
        store_shifted(
            c_sh[layer - 1], slope * value, rows, lane, x_first - halo + 2 * pair, keep
        )

    halo = plan.halo_u[1]
    for pair in range(plan.x(halo) // 2):
        lane = pair * 2 * LANES
        forward_tail(one_channel(first_sh, w_first, lane), 1, 0, plan.z(halo), pair, lane)
    for layer in range(2, layers + 1):
        halo = plan.halo_u[layer]
        size, starts = plan.starts(plan.z(halo))
        for start in starts:
            values = many_channels(
                u_sh[layer - 2], w_fwd[layer - 2], start, size, plan.x(halo) // 2
            )
            for pair, value in enumerate(values):
                forward_tail(value, layer, start, size, pair, pair * 2 * LANES)

    def own_taps(source, halo):
        rows = slice((halo - 1) * c, (halo + zs + 1) * c)
        pieces = [
            source[dy, rows, (halo - 1 + dx) * LANES : (halo - 1 + dx + xs) * LANES]
            for dx in range(3)
            for dy in range(3)
        ]
        return jnp.concatenate(pieces, axis=0)

    top = plan.halo_u[layers]
    taps = own_taps(u_sh[layers - 1], top)
    last = jnp.dot(w_out[:, : taps.shape[0]], taps, preferred_element_type=f32)
    new_image[...] = em_own[...] + last[:zs, :]

    halo = plan.halo_c[-1]

    for pair in range(plan.x(halo) // 2):
        lane = pair * 2 * LANES
        backward_tail(one_channel(last_sh, w_top, lane), layers, 0, plan.z(halo), pair, lane)
    for layer in range(layers - 1, 0, -1):
        halo = plan.halo_c[layer - 1]
        size, starts = plan.starts(plan.z(halo))
        for start in starts:
            values = many_channels(c_sh[layer], w_bwd[layer - 1], start, size, plan.x(halo) // 2)
            for pair, value in enumerate(values):
                backward_tail(value, layer, start, size, pair, pair * 2 * LANES)
    taps = own_taps(c_sh[0], plan.halo_c[0])
    down = jnp.dot(w_back[:, : taps.shape[0]], taps, preferred_element_type=f32)
    em_grad[...] = cot_own[...] + down[:zs, :]

    def own_rows(source, halo, plane):
        return source[1, (halo + plane) * c : (halo + plane + 1) * c, halo * LANES : (halo + xs) * LANES]

    def against(cells, taps):
        return lax.dot_general(cells, taps, (((1,), (1,)), ((), ())), preferred_element_type=f32)

    block = round_up(27 * c, LANES) // LANES
    for layer in range(2, layers + 1):
        source, halo = u_sh[layer - 2], plan.halo_u[layer - 1]
        total = None
        for plane in range(zs):
            first = halo - 1 + plane
            pieces = [
                source[
                    dy,
                    (first + dz) * c : (first + dz + 1) * c,
                    (halo - 1 + dx) * LANES : (halo - 1 + dx + xs) * LANES,
                ]
                for dz in range(3)
                for dx in range(3)
                for dy in range(3)
            ]
            pieces.append(jnp.zeros((block * LANES - 27 * c, xs * LANES), bf16))
            cells = own_rows(c_sh[layer - 1], plan.halo_c[layer - 1], plane)
            term = against(cells, jnp.concatenate(pieces, axis=0))
            total = term if total is None else total + term
        for k in range(block):
            at = ((layer - 2) * block + k) * c
            grads[at : at + c, :] = total[:, k * LANES : (k + 1) * LANES]

    def thin(source, halo, lead, cells_of, at):
        row = lead + halo - 1
        pieces = [
            source[dy, row : row + 8, (halo - 1 + dx) * LANES : (halo - 1 + dx + xs) * LANES]
            for dx in range(3)
            for dy in range(3)
        ]
        pieces.append(jnp.zeros((LANES - 72, xs * LANES), f32))
        taps = jnp.concatenate(pieces, axis=0).astype(bf16)
        total = None
        for plane in range(zs):
            term = against(cells_of(plane), taps)
            if plane:
                term = pltpu.roll(term, LANES - plane, 1)
            total = term if total is None else total + term
        grads[at : at + c, :] = total

    thin(
        first_sh,
        plan.halo_in,
        plan.lead_in,
        lambda plane: own_rows(c_sh[0], plan.halo_c[0], plane),
        mids * block * c,
    )
    thin(
        last_sh,
        plan.halo_last,
        plan.lead_last,
        lambda plane: own_rows(u_sh[layers - 1], top, plane),
        (mids * block + 1) * c,
    )
    used = (mids * block + 2) * c
    if used < grads.shape[0]:
        grads[used:, :] = jnp.zeros((grads.shape[0] - used, LANES), f32)


def prepared_weights(plan, w_in, w_mid, w_out):
    c, mids = plan.c, plan.layers - 1
    bf16 = jnp.bfloat16

    def banded(halo):
        size, _ = plan.starts(plan.z(halo))
        return (3 * size * c, round_up(3 * (size + 2) * c, LANES))

    last = (8, round_up(9 * (plan.zs + 2) * c, LANES))
    shapes = [
        (plan.z(plan.halo_u[1]) * c, round_up(9 * plan.rows_in, LANES)),
        (plan.z(plan.halo_c[-1]) * c, round_up(9 * plan.rows_last, LANES)),
        last,
        last,
    ]
    shapes += [banded(plan.halo_u[k + 2]) for k in range(mids)]
    shapes += [banded(plan.halo_c[k]) for k in range(mids)]
    vmem = pl.BlockSpec(memory_space=pltpu.VMEM)
    return pl.pallas_call(
        lambda *refs: prepare_kernel(plan, *refs),
        out_shape=[jax.ShapeDtypeStruct(shape, bf16) for shape in shapes],
        in_specs=[vmem] * 3,
        out_specs=[vmem] * len(shapes),
        compiler_params=pltpu.CompilerParams(vmem_limit_bytes=SMALL_VMEM_BYTES),
        name="prepare_weights",
    )(
        jnp.transpose(w_in, (2, 3, 4, 1, 0)).reshape(27, c),
        jnp.transpose(w_mid, (0, 3, 4, 5, 1, 2)).reshape(mids * 27, c, c),
        jnp.transpose(w_out, (2, 3, 4, 0, 1)).reshape(27, c),
    )


def network(plan, grid, position, received, em_own, cot_own, weights, packed_rows):
    layers, c = plan.layers, plan.c
    f32, bf16 = jnp.float32, jnp.bfloat16
    own = jax.ShapeDtypeStruct((plan.zs, plan.xs * LANES), f32)
    scratch = [
        pltpu.VMEM((3, plan.rows_in, plan.x(plan.halo_in) * LANES), f32),
        pltpu.VMEM((3, plan.rows_last, plan.x(plan.halo_last) * LANES), f32),
    ]

    def region(halo, lead=()):
        return (*lead, plan.z(halo) * c, plan.x(halo) * LANES)

    scratch += [pltpu.VMEM(region(plan.halo_u[l], (3,)), bf16) for l in range(1, layers + 1)]
    scratch += [pltpu.VMEM(region(plan.halo_c[l - 1]), f32) for l in range(1, layers + 1)]
    scratch += [pltpu.VMEM(region(plan.halo_c[l - 1], (3,)), bf16) for l in range(1, layers + 1)]
    vmem = pl.BlockSpec(memory_space=pltpu.VMEM)
    scratch += [
        pltpu.VMEM((plan.rows_in, plan.x(plan.halo_in) * LANES), f32),
        pltpu.VMEM((plan.rows_last, plan.x(plan.halo_last) * LANES), f32),
    ]
    operands = (position, received, em_own, cot_own, *weights)
    return pl.pallas_call(
        lambda *refs: network_kernel(plan, grid, *refs),
        out_shape=[own, own, jax.ShapeDtypeStruct((packed_rows, LANES), f32)],
        in_specs=[pl.BlockSpec(memory_space=pltpu.SMEM)] + [vmem] * (len(operands) - 1),
        out_specs=[vmem] * 3,
        scratch_shapes=scratch,
        compiler_params=pltpu.CompilerParams(vmem_limit_bytes=VMEM_BYTES),
        name="network",
    )(*operands)


def image_kernel(plan, grid, copies, pos, parts, sent, em_own, cot_own):
    zs, xs, halo, outer = plan.zs, plan.xs, plan.halo_in, plan.halo_last
    reach = -(-halo // (xs * CORES))
    span = (2 * reach + 1) * CORES * xs
    x_first = pos[1]
    core = lax.rem(lax.div(x_first, xs), CORES)
    row = x_first - (core + reach * CORES) * xs + lax.broadcasted_iota(jnp.int32, (span, LANES), 0)
    good = jnp.logical_and(row >= 0, row < grid[1])

    def near(field, z):
        pieces = []
        for chip in range(2 * reach + 1):
            at = zs * span + (chip * 3 + field) * zs * xs + z * xs
            pieces += [parts[k, at : at + xs, :] for k in range(CORES)]
        return jnp.concatenate(pieces, axis=0)

    def window(rows, halo):
        first = reach * CORES * xs - halo
        count = xs + 2 * halo
        taken = rows[first : first + count]
        for k in range(1, CORES):
            taken = jnp.where(core == k, rows[first + k * xs : first + k * xs + count], taken)
        return taken

    for z in range(zs):
        back = parts[0, z * span : (z + 1) * span, :]
        for k in range(1, CORES):
            back = back + parts[k, z * span : (z + 1) * span, :]
        em = window(jnp.where(good, near(0, z) * back / near(1, z), 0.0), halo)
        cot = window(jnp.where(good, near(2, z), 0.0), outer)
        both = jnp.concatenate([em, cot], axis=0).astype(jnp.bfloat16)
        for k in range(copies):
            sent[k, z] = both
        for x in range(xs):
            lanes = slice(x * LANES, (x + 1) * LANES)
            em_own[z : z + 1, lanes] = em[halo + x : halo + x + 1, :]
            cot_own[z : z + 1, lanes] = cot[outer + x : outer + x + 1, :]


def image_and_halo(plan, grid, copies, position, parts):
    f32 = jnp.float32
    rows = plan.x(plan.halo_in) + plan.x(plan.halo_last)
    own = jax.ShapeDtypeStruct((plan.zs, plan.xs * LANES), f32)
    vmem = pl.BlockSpec(memory_space=pltpu.VMEM)
    return pl.pallas_call(
        lambda *refs: image_kernel(plan, grid, copies, *refs),
        out_shape=[jax.ShapeDtypeStruct((copies, plan.zs, rows, LANES), jnp.bfloat16), own, own],
        in_specs=[pl.BlockSpec(memory_space=pltpu.SMEM), vmem],
        out_specs=[vmem] * 3,
        compiler_params=pltpu.CompilerParams(vmem_limit_bytes=SMALL_VMEM_BYTES),
        name="image_and_halo",
    )(position, parts)


def grad_rows(plan):
    return ((plan.layers - 1) * (round_up(27 * plan.c, LANES) // LANES) + 2) * plan.c


def unpack_kernel(plan, factor, halves, grad_in, grad_mid, grad_out):
    c, mids = plan.c, plan.layers - 1
    block, per, rows = round_up(27 * c, LANES) // LANES, LANES // c, halves.shape[2]

    def packed(first):
        pieces = []
        for at in range(first, first + c, 8):
            slab, inner = divmod(at, CORES * rows)
            core, row = divmod(inner, rows)
            pieces.append(halves[core, slab, row : row + 8, :])
        return jnp.concatenate(pieces, axis=0) * factor

    for layer in range(mids):
        for k in range(block):
            lanes = packed((layer * block + k) * c)
            for tap in range(min(per, 27 - k * per)):
                grad_mid[layer * 27 + k * per + tap] = lanes[:, tap * c : (tap + 1) * c]
    for index, out in enumerate((grad_in, grad_out)):
        taps = packed((mids * block + index) * c).T
        for dz in range(3):
            for k in range(9):
                tap = dz * 9 + k
                out[26 - tap if index else tap] = taps[k * 8 + dz : k * 8 + dz + 1, :]


def unpack_grads(plan, halves, factor):
    c, mids = plan.c, plan.layers - 1
    f32 = jnp.float32
    thin = jax.ShapeDtypeStruct((27, 1, c), f32)
    vmem = pl.BlockSpec(memory_space=pltpu.VMEM)
    grad_in, mid, grad_out = pl.pallas_call(
        lambda *refs: unpack_kernel(plan, factor, *refs),
        out_shape=[thin, jax.ShapeDtypeStruct((mids * 27, c, c), f32), thin],
        in_specs=[vmem],
        out_specs=[vmem] * 3,
        compiler_params=pltpu.CompilerParams(vmem_limit_bytes=SMALL_VMEM_BYTES),
        name="unpack_gradients",
    )(halves)
    mid = jnp.transpose(mid.reshape(mids, 3, 3, 3, c, c), (0, 4, 5, 1, 2, 3))
    grad_in = jnp.transpose(grad_in.reshape(3, 3, 3, 1, c), (4, 3, 0, 1, 2))
    grad_out = jnp.transpose(grad_out.reshape(3, 3, 3, 1, c), (3, 4, 0, 1, 2))
    return grad_in, mid, grad_out


CORES = 2


def along_chips(axis):
    count = lax.axis_size(axis)
    return [list(range(core, count, CORES)) for core in range(CORES)]


def within_chip(axis):
    count = lax.axis_size(axis)
    return [list(range(first, first + CORES)) for first in range(0, count, CORES)]


def to_all(value, axis, groups=None):
    count = lax.axis_size(axis) if groups is None else len(groups[0])
    copies = jnp.broadcast_to(value[None], (count, *value.shape))
    return lax.all_to_all(copies, axis, 0, 0, tiled=True, axis_index_groups=groups)


def pair_gather(value):
    return lax.all_gather(value, "sector", axis_index_groups=within_chip("sector"))


def summed_everywhere(packed, slabs, beside):
    chips = along_chips("sector")
    core = lax.rem(lax.axis_index("sector"), CORES)
    share = packed.shape[0] // slabs
    parts = packed.reshape(slabs, share, LANES)
    own = jnp.sum(lax.all_to_all(parts, "slab", 0, 0, tiled=True), axis=0)
    both = pair_gather(own)
    own = both[0] + both[1]
    half = lax.dynamic_slice_in_dim(own, core * (share // CORES), share // CORES, 0)
    half = to_all(half.astype(jnp.bfloat16), "sector", chips)
    half, beside = lax.optimization_barrier((half, beside))
    half = jnp.sum(half.astype(jnp.float32), axis=0)
    return pair_gather(to_all(half, "slab")), beside


def small_call(kernel, name, shapes, operands, scalars):
    vmem = pl.BlockSpec(memory_space=pltpu.VMEM)
    smem = pl.BlockSpec(memory_space=pltpu.SMEM)
    return pl.pallas_call(
        kernel,
        out_shape=shapes,
        in_specs=[smem] * scalars + [vmem] * (len(operands) - scalars),
        out_specs=vmem,
        compiler_params=pltpu.CompilerParams(vmem_limit_bytes=SMALL_VMEM_BYTES),
        name=name,
    )(*operands)


def message_kernel(image, cols, out):
    f32 = jnp.float32
    zs = image.shape[0]
    rows = [image[z] for z in range(zs)]
    numbers = cols[...].astype(f32)
    rows.append(jnp.concatenate([numbers, jnp.zeros((1, LANES - numbers.shape[1]), f32)], axis=1))
    used = sum(part.shape[0] for part in rows)
    if out.shape[1] > used:
        rows.append(jnp.zeros((out.shape[1] - used, LANES), f32))
    message = jnp.concatenate(rows, axis=0).astype(out.dtype)
    for k in range(out.shape[0]):
        out[k] = message


def padded_rows(rows):
    short = round_up(rows.shape[0], 16) - rows.shape[0]
    if short:
        rows = jnp.concatenate([rows, jnp.zeros((short, rows.shape[1]), rows.dtype)], axis=0)
    return rows


def backward_kernel(block_len, rows, count, every, measured, background, values, out):
    f32, bf16 = jnp.float32, jnp.bfloat16
    slots, row_len, _ = values.shape
    line_blocks = measured.shape[1]
    terms = jnp.concatenate([every[k] for k in range(every.shape[0])], axis=0)
    number = lax.broadcasted_iota(jnp.int32, (terms.shape[0], line_blocks), 1).astype(f32)
    placing = jnp.where(terms[:, row_len : row_len + 1] == number, 1.0, 0.0)
    projection = lax.dot_general(
        placing,
        terms,
        (((0,), (0,)), ((), ())),
        precision=lax.Precision.HIGHEST,
        preferred_element_type=f32,
    )[:, :row_len]
    ratio = (measured[0] / (projection + background[0])).astype(bf16)
    number = lax.broadcasted_iota(jnp.int32, (1, line_blocks), 1)
    chosen = [jnp.where(number == rows[0, k], 1.0, 0.0) for k in range(slots)]
    chosen = padded_rows(jnp.concatenate(chosen, axis=0)).astype(bf16)
    ratios = jnp.dot(chosen, ratio, preferred_element_type=f32).astype(bf16)
    lines = []
    for k in range(slots):
        sums = jnp.dot(ratios, values[k], preferred_element_type=f32)
        weight = jnp.where(k < count[0, 0], 1.0 / block_len, 0.0)
        lines.append(sums[k : k + 1] * weight)
    lines = jnp.concatenate(lines, axis=0)
    for k in range(out.shape[0]):
        out[k] = lines


def shards(
    image,
    sensitivity,
    tile_values,
    tile_rows,
    tile_cols,
    tile_count,
    measured,
    background,
    w_in,
    w_mid,
    w_out,
    cotangent,
):
    f32, bf16 = jnp.float32, jnp.bfloat16
    highest = lax.Precision.HIGHEST
    sectors, slabs = lax.axis_size("sector"), lax.axis_size("slab")
    sector, slab = lax.axis_index("sector"), lax.axis_index("slab")
    zs, xs, ys = image.shape
    block_len = xs * ys
    row_len = measured.shape[2]
    slots = tile_rows.shape[1]
    plan = Plan(zs, xs, w_in.shape[0], w_mid.shape[0] + 1)
    grid = (zs * slabs, xs * sectors)

    cells = zs * xs
    chips = along_chips("sector")
    message = jax.ShapeDtypeStruct((len(chips[0]), round_up(cells + 1, 8), ys), bf16)
    message = small_call(message_kernel, "first_message", message, (image, tile_cols), 0)
    from_chips = lax.all_to_all(message, "sector", 0, 0, tiled=True, axis_index_groups=chips)
    every_cols = from_chips[:, cells, :slots].astype(f32).reshape(-1)
    got = pair_gather(from_chips[:, :cells])
    got = jnp.transpose(got.reshape(CORES, len(chips[0]), zs, xs, ys), (2, 1, 0, 3, 4))
    blocks = got.reshape(zs * sectors, block_len)

    fields = jnp.concatenate([field.reshape(cells, ys) for field in (image, sensitivity, cotangent)], axis=0)
    fields = jnp.pad(fields, ((0, round_up(3 * cells, 8) - 3 * cells), (0, 0)))
    fields, from_chips = lax.optimization_barrier((fields, from_chips))
    reach = -(-plan.halo_in // (xs * CORES))
    near_fields = []
    for chip in range(-reach, reach + 1):
        step = chip * CORES
        pairs = [(k + step, k) for k in range(sectors) if 0 <= k + step < sectors]
        near_fields.append(lax.ppermute(fields, "sector", pairs) if chip else fields)
    near_fields = jnp.concatenate([field[: 3 * cells] for field in near_fields], axis=0)

    values = tile_values[0]
    weight = (jnp.arange(slots) < tile_count[0, 0]).astype(f32) / block_len
    forward = jnp.einsum("krv,kv->kr", values, blocks[tile_cols[0]], preferred_element_type=f32)
    forward = forward * weight[:, None]
    lined = jnp.concatenate([forward, tile_rows[0].astype(f32)[:, None]], axis=1)
    lined = jnp.pad(lined, ((0, 0), (0, LANES - row_len - 1)))
    lined, *kernels = lax.optimization_barrier((lined, w_in, w_mid, w_out))
    weights = prepared_weights(plan, *kernels)
    every = to_all(lined, "slab")

    backward = small_call(
        lambda *refs: backward_kernel(block_len, *refs),
        "back_terms",
        jax.ShapeDtypeStruct((len(chips[0]), slots, block_len), f32),
        (tile_rows, tile_count, every, measured, background, values),
        2,
    )
    backward, weights = lax.optimization_barrier((backward, weights))
    every_back = lax.all_to_all(backward, "sector", 0, 0, tiled=True, axis_index_groups=chips)
    every_back = every_back.reshape(-1, block_len)
    core = lax.rem(sector, CORES)
    span = (2 * reach + 1) * CORES
    near = sector - core - reach * CORES + jnp.arange(span)
    wanted = (jnp.arange(zs)[:, None] * sectors + near[None, :]).astype(f32)
    good = jnp.logical_and(near >= 0, near < sectors)
    wanted = jnp.where(good[None, :], wanted, -1.0).reshape(-1)
    owning = (every_cols[None, :] == wanted[:, None]).astype(f32)
    of_core = jnp.dot(owning, every_back, precision=highest).reshape(-1, ys)
    of_cores = pair_gather(jnp.concatenate([of_core, near_fields], axis=0))
    position = jnp.stack([slab * zs, sector * xs]).astype(jnp.int32)
    to_send, em_own, cot_own = image_and_halo(plan, grid, slabs, position, of_cores)

    received = lax.all_to_all(to_send, "slab", 0, 0, tiled=True)
    received = received.reshape(zs * slabs, *received.shape[2:])
    new_image, em_grad, packed = network(
        plan,
        grid,
        position,
        received,
        em_own,
        cot_own,
        weights,
        round_up(grad_rows(plan), slabs * CORES * 8),
    )
    new_image = new_image.reshape(zs, xs, ys)
    em_grad = em_grad.reshape(zs, xs, ys)
    halves, new_image = summed_everywhere(packed, slabs, new_image)
    factor = 1.0 / math.sqrt(grid[0] * grid[1] * ys)
    grad_in, grad_mid, grad_out = unpack_grads(plan, halves, factor)
    return (
        new_image,
        em_grad,
        grad_in,
        grad_mid,
        grad_out,
    )


def solution(mesh):
    placed = (
        P("slab", "sector", None),
        P("slab", "sector", None),
        P("sector", "slab", None, None),
        P("sector", "slab"),
        P("sector", "slab"),
        P("sector", "slab"),
        P("sector", None, None),
        P("sector", None, None),
        P(),
        P(),
        P(),
        P("slab", "sector", None),
    )
    return jax.shard_map(
        shards,
        mesh=mesh,
        in_specs=placed,
        out_specs=(P("slab", "sector", None), P("slab", "sector", None), P(), P(), P()),
        check_vma=False,
    )
```
